128 devices in a mesh: row: 16 (over y_lo, z, core), col: 8 (over x, y_hi).
Axes of the slice: x: 4, y: 4 (y_hi: 2, y_lo: 2; y = y_hi * 2 + y_lo), z: 4, core: 2. Of those that a mesh axis runs over, the one named last changes fastest.
Arguments:
- front: float32 [8, 2048, 16, 1024], P(None, 'row', None, 'col')
- child_blocks: float32 [2, 4, 2048, 8, 1024], P(None, None, 'row', None, 'col')
- child_map: int32 [2, 64], replicated, may hold values from 0 to 127, as said below
Outputs:
- factored: float32 [8, 2048, 16, 1024], P(None, 'row', None, 'col')
The draws below stay inside these ranges and needn't reach their ends.
Inputs may be any that keep to these rules, and one draw needn't show every extreme that they name: Each child's entries are distinct. For each child h and each k below 4, (child_map[h, t] - t) mod 16 is the same for all t with t // 16 = k. Of the tiles t with one value of t mod 16, over both children, at most 1 share one value of child_map mod 16; of one child's tiles t with one value of t mod 8, at most 2 share one value of child_map mod 8; both bounds are reached in every draw.
All inputs are finite; a program needn't handle non-finite values.
Results may differ from the reference program's by a relative error of at most 0.0001.
Values sent between devices are 32-bit elements; how exact they have to be, the bound alone decides.
No kernel may reach another device: no remote copies, remote signals or barrier semaphores. Data moves between devices by JAX's collectives and lax.ppermute only.
A program may use at most 192 MiB of HBM per device.

```python
import math
import jax
import jax.numpy as jnp
from jax import lax

FRONT_ORDER = 16384
CHILD_ORDER = 8192
TILE_SIZE = 128
PANEL_WIDTH = 512
PANELS = 2
FRONT_ROW_TILES = 8
CHILD_ROW_TILES = 4
N_ROW = 16
N_COL = 8


gram_width = 512


gram_norm = 1.0 / math.sqrt(512.0)


def gram_matrix(factors):
    gram = jnp.dot(factors, factors.T, precision=lax.Precision.HIGHEST, preferred_element_type=jnp.float32) * gram_norm
    return (gram + gram.T) * 0.5


def draw_front(key, part):
    order = FRONT_ORDER
    first, second, third = jax.random.split(jax.random.fold_in(key, 11), 3)
    factors = jax.random.normal(first, (order, gram_width), jnp.float32)
    scales = jnp.exp(jax.random.uniform(second, (order,), jnp.float32, math.log(0.7), math.log(1.4)))
    gram = gram_matrix(factors * scales[:, None])
    shift = jax.random.uniform(third, (order,), jnp.float32, 8.0, 16.0)
    on_diagonal = jnp.arange(order)[:, None] == jnp.arange(order)[None, :]
    full = gram + jnp.where(on_diagonal, shift[:, None], jnp.float32(0.0))
    return full.reshape(order // (TILE_SIZE * N_ROW), TILE_SIZE * N_ROW, order // (TILE_SIZE * N_COL), TILE_SIZE * N_COL)


def draw_child_blocks(key, part):
    order = CHILD_ORDER
    on_diagonal = jnp.arange(order)[:, None] == jnp.arange(order)[None, :]
    blocks = []
    for child in range(2):
        first, second, third = jax.random.split(jax.random.fold_in(key, 23 + child), 3)
        factors = jax.random.normal(first, (order, gram_width), jnp.float32)
        scales = jnp.exp(jax.random.uniform(second, (order,), jnp.float32, math.log(0.7), math.log(1.4)))
        added = jax.random.uniform(third, (order,), jnp.float32, 1.0, 2.0)
        gram = gram_matrix(factors * scales[:, None])
        blocks.append(gram + jnp.where(on_diagonal, added[:, None], jnp.float32(0.0)))
    stacked = jnp.stack(blocks)
    return stacked.reshape(2, order // (TILE_SIZE * N_ROW), TILE_SIZE * N_ROW, order // (TILE_SIZE * N_COL), TILE_SIZE * N_COL)


def draw_child_map(key, part):
    row_count = N_ROW
    col_count = N_COL
    per_child = CHILD_ROW_TILES
    front_rows = FRONT_ROW_TILES
    child_tiles = CHILD_ORDER // TILE_SIZE
    first, second, third = jax.random.split(jax.random.fold_in(key, 7), 3)
    if col_count > 1:
        head_values = [0, col_count - 1]
    else:
        head_values = [0]
    rest_values = [value for value in range(col_count) if value not in head_values]
    head_array = jnp.array(head_values, dtype=jnp.int32)
    if len(rest_values) > 0:
        rest_array = jax.random.permutation(first, jnp.array(rest_values, dtype=jnp.int32))
        low_table = jnp.concatenate([head_array, rest_array])
    else:
        low_table = head_array
    lifted = jax.random.randint(second, (), 0, row_count // col_count)
    serial = jnp.arange(2 * per_child)
    base = col_count * ((serial // col_count + lifted) % (row_count // col_count)) + low_table[serial % col_count]
    shifts = (row_count // 2 - (base - base[0])) % row_count
    keys = jax.random.split(third, 2 * row_count)
    orders = jax.vmap(lambda single: jax.random.permutation(single, front_rows))(keys).reshape(2, row_count, front_rows)
    tiles = jnp.arange(child_tiles)
    residue = tiles % row_count
    level = tiles // row_count
    result = []
    for child in range(2):
        shift = shifts[child * per_child + level]
        owner = (residue + shift) % row_count
        local = orders[child, owner, level]
        result.append(row_count * local + owner)
    return jnp.stack(result).astype(jnp.int32)


def setup_inputs(seed: int = 0) -> dict:
    key_of = jax.random.split(jax.random.key(seed), 4)
    front = draw_front(jax.random.fold_in(key_of[3], 71), 0)
    child_blocks = draw_child_blocks(jax.random.fold_in(key_of[3], 71), 0)
    child_map = draw_child_map(jax.random.fold_in(key_of[3], 71), 0)
    return {"front": front, "child_blocks": child_blocks, "child_map": child_map}


def reference(front, child_blocks, child_map):
    square = TILE_SIZE
    order = FRONT_ORDER
    tile_count = order // square
    child_count = CHILD_ORDER // square
    tiled = front.reshape(tile_count, square, tile_count, square)
    for child in range(2):
        block = child_blocks[child].reshape(child_count, square, child_count, square)
        block = jnp.transpose(block, (0, 2, 1, 3))
        target = child_map[child].astype(jnp.int32)
        tiled = tiled.at[target[:, None], :, target[None, :], :].add(block)
    matrix = tiled.reshape(order, order)
    line_index = jnp.arange(order)
    for panel in range(PANELS):
        start = panel * PANEL_WIDTH
        stop = start + PANEL_WIDTH
        lower = jnp.linalg.cholesky(matrix[start:stop, start:stop])
        factor = jax.scipy.linalg.solve_triangular(lower, matrix[:, start:stop].T, lower=True).T
        factor = jnp.where(line_index[:, None] >= start, factor, jnp.float32(0.0))
        product = jnp.dot(factor.astype(jnp.float32), factor.T.astype(jnp.float32), precision=lax.Precision.HIGHEST, preferred_element_type=jnp.float32)
        trailing = line_index >= stop
        matrix = matrix - jnp.where(trailing[:, None] & trailing[None, :], product, jnp.float32(0.0))
        matrix = matrix.at[:, start:stop].set(jnp.where(line_index[:, None] >= start, factor, matrix[:, start:stop]))
    return matrix.reshape(front.shape)
```

```python
import functools

import jax
import jax.numpy as jnp
from jax import lax
from jax.experimental import pallas as pl
from jax.experimental.pallas import tpu as pltpu
from jax.sharding import PartitionSpec as P

T = 128
W = 1024
F32 = jnp.float32
BF16 = jnp.bfloat16
HIGHEST = lax.Precision.HIGHEST
ROW_AT = 128
COL_AT = 129
VMEM = 58 * 1024 * 1024


def params(**kw):
    return pltpu.CompilerParams(vmem_limit_bytes=VMEM, **kw)


def shift(meta, h, k):
    return meta[h * 64 + 16 * k] & 15


def source_row(meta, h, ka):
    return (meta[ROW_AT] - shift(meta, h, ka)) & 15


def local_row(meta, h, ka):
    return meta[h * 64 + source_row(meta, h, ka) + 16 * ka] >> 4


def level_of(meta, h, a):
    ka = jnp.int32(0)
    found = jnp.int32(0)
    for k in range(4):
        hit = local_row(meta, h, k) == a
        ka = jnp.where(hit, k, ka)
        found = jnp.where(hit, 1, found)
    return ka, found


def dest_col(meta, h, kb):
    return (meta[COL_AT] + shift(meta, h, kb)) & 7


def source_col(meta, h, kb):
    return (meta[COL_AT] - shift(meta, h, kb)) & 7


def local_col(meta, h, kb, i):
    return meta[h * 64 + source_col(meta, h, kb) + 8 * (2 * kb + i)] >> 3


def split(x):
    hi = x.astype(BF16)
    return hi, (x - hi.astype(F32)).astype(BF16)


def dot(a, b, dims=((1,), (0,)), precision=None):
    return lax.dot_general(a, b, (dims, ((), ())), precision=precision, preferred_element_type=F32)


NT = ((1,), (1,))


def dot3(a, b, dims=((1,), (0,))):
    return dot(a[0], b[0], dims) + (dot(a[0], b[1], dims) + dot(a[1], b[0], dims))


def pack_rows_kernel(meta, child_ref, out_ref):
    flat = child_ref.reshape(T * 8, T)
    for j in range(8):
        out_ref[0, j] = flat[pl.ds(j, T, stride=8), :]


def pack_rows(meta, child):
    return pl.pallas_call(
        pack_rows_kernel,
        grid_spec=pltpu.PrefetchScalarGridSpec(
            num_scalar_prefetch=1,
            grid=(2, 4),
            in_specs=[pl.BlockSpec((None, None, T, 8, T), lambda h, k, m: (h, k, 0, 0, 0))],
            out_specs=pl.BlockSpec(
                (1, 8, T, T), lambda h, k, m: ((m[ROW_AT] + shift(m, h, k)) & 15, 0, 0, 0)
            ),
        ),
        out_shape=jax.ShapeDtypeStruct((16, 8, T, T), F32),
        compiler_params=params(),
        name="pack_rows",
    )(meta, child)


def pack_cols_kernel(levels, meta, arrived, out, sems):
    copies = []
    for h in range(2):
        for lev in range(levels):
            if levels == 1:
                ka, _ = level_of(meta, h, 0)
            else:
                ka = lev
            src = source_row(meta, h, ka)
            for kb in range(4):
                copies.append(
                    pltpu.make_async_copy(
                        arrived.at[src, pl.ds(2 * kb, 2)],
                        out.at[dest_col(meta, h, kb), h, lev],
                        sems.at[len(copies)],
                    )
                )
    for c in copies:
        c.start()
    for c in copies:
        c.wait()


def pack_cols(meta, arrived, levels):
    return pl.pallas_call(
        functools.partial(pack_cols_kernel, levels),
        in_specs=[pl.BlockSpec(memory_space=pltpu.SMEM), pl.BlockSpec(memory_space=pl.ANY)],
        out_specs=pl.BlockSpec(memory_space=pl.ANY),
        out_shape=jax.ShapeDtypeStruct((8, 2, levels, 2, T, T), F32),
        scratch_shapes=[pltpu.SemaphoreType.DMA((8 * levels,))],
        name=f"pack_cols_{levels}",
    )(meta, arrived)


def first_row_kernel(meta, front_ref, got_ref, out_ref):
    flat = front_ref.reshape(T * 16, T)
    for lc in range(16):
        out_ref[(lc % 2) * 8 + lc // 2] = flat[pl.ds(lc, T, stride=16), :]
    for h in range(2):
        _, found = level_of(meta, h, 0)

        @pl.when(found == 1)
        def _():
            for kb in range(4):
                src = source_col(meta, h, kb)
                for i in range(2):
                    lc = local_col(meta, h, kb, i)
                    at = (lc & 1) * 8 + (lc >> 1)
                    out_ref[at] = out_ref[at] + got_ref[src, h, 0, i]


def first_row(meta, front, got):
    return pl.pallas_call(
        first_row_kernel,
        grid_spec=pltpu.PrefetchScalarGridSpec(
            num_scalar_prefetch=1,
            grid=(1,),
            in_specs=[
                pl.BlockSpec((None, T, 16, T), lambda i, m: (0, 0, 0, 0)),
                pl.BlockSpec((8, 2, 1, 2, T, T), lambda i, m: (0, 0, 0, 0, 0, 0)),
            ],
            out_specs=pl.BlockSpec((16, T, T), lambda i, m: (0, 0, 0)),
        ),
        out_shape=jax.ShapeDtypeStruct((16, T, T), F32),
        compiler_params=params(),
        name="first_row",
    )(meta, front, got)


def invert_kernel(pieces, hi_ref, lo_ref, a_ref, t_ref, l_ref):
    for q in range(8):
        for c in range(8):
            for half in range(2):
                a_ref[q * T + half * 64 : q * T + half * 64 + 64, c * T : (c + 1) * T] = pieces[
                    q + 8 * half, c
                ]
    t_ref[...] = jnp.zeros_like(t_ref)
    sub = lax.broadcasted_iota(jnp.int32, (8, T), 0)
    lane = lax.broadcasted_iota(jnp.int32, (8, T), 1)

    def step(k, _):
        at = pl.multiple_of(k * T, T)
        s = [a_ref[pl.ds(at + 8 * b, 8), pl.ds(at, T)] for b in range(16)]
        t = [jnp.where(lane == sub + 8 * b, F32(1), F32(0)) for b in range(16)]
        for j in range(T):
            b0, i0 = divmod(j, 8)
            pivot = s[b0][i0 : i0 + 1, j : j + 1]
            r = lax.rsqrt(pivot)
            r = r * (1.5 - 0.5 * pivot * r * r)
            u = jnp.broadcast_to(s[b0][i0 : i0 + 1, :], (8, T)) * r
            w = jnp.broadcast_to(t[b0][i0 : i0 + 1, :], (8, T)) * r
            for b in range(b0, 16):
                v = jnp.broadcast_to(s[b][:, j : j + 1], (8, T)) * r
                if b == b0:
                    v = jnp.where(sub > i0, v, F32(0))
                    t[b] = jnp.where(sub == i0, w, t[b] - v * w)
                else:
                    t[b] = t[b] - v * w
                s[b] = s[b] - v * u
        kinv = jnp.concatenate(t, axis=0)
        for kk in range(8):

            @pl.when(k == kk)
            def _():
                lo, hi = kk * T, (kk + 1) * T
                if kk:
                    t_ref[lo:hi, :lo] = dot(kinv, t_ref[lo:hi, :lo], precision=HIGHEST)
                t_ref[lo:hi, lo:hi] = kinv
                if kk < 7:
                    col = dot(a_ref[hi:, lo:hi], kinv, NT, precision=HIGHEST)
                    l_ref[hi:, :] = col
                    for n0 in range(hi, W, T):
                        a_ref[n0:, n0 : n0 + T] = a_ref[n0:, n0 : n0 + T] - dot(
                            l_ref[n0:, :], l_ref[n0 : n0 + T, :], NT, precision=HIGHEST
                        )
                    t_ref[hi:, :hi] = t_ref[hi:, :hi] - dot(
                        l_ref[hi:, :], t_ref[lo:hi, :hi], precision=HIGHEST
                    )

        return 0

    lax.fori_loop(0, 8, step, 0)
    hi_ref[...], lo_ref[...] = split(t_ref[...])


def invert(pieces):
    return pl.pallas_call(
        invert_kernel,
        out_shape=[jax.ShapeDtypeStruct((W, W), BF16)] * 2,
        scratch_shapes=[
            pltpu.VMEM((W, W), F32),
            pltpu.VMEM((W, W), F32),
            pltpu.VMEM((W, T), F32),
        ],
        compiler_params=params(),
        cost_estimate=pl.CostEstimate(flops=80_000_000_000, bytes_accessed=8 << 20, transcendentals=0),
        name="invert",
    )(pieces)


B = 256


def solve_cols_kernel(ihi, ilo, x_ref, ohi, olo):
    x = jnp.concatenate(
        [jnp.concatenate([x_ref[q, 0], x_ref[q, 1]], axis=1) for q in range(8)], axis=0
    )
    xs = split(x)
    for k in range(W // B):
        n = (k + 1) * B
        rows = slice(k * B, n)
        y = dot3((ihi[rows, :n], ilo[rows, :n]), (xs[0][:n], xs[1][:n]))
        ohi[rows, :], olo[rows, :] = split(y)


def solve_cols(inverse, x):
    whole = pl.BlockSpec((W, W), lambda i: (0, 0))
    out = pl.BlockSpec((W, B), lambda i: (0, i))
    return pl.pallas_call(
        solve_cols_kernel,
        grid=(8,),
        in_specs=[
            whole,
            whole,
            pl.BlockSpec((None, 8, 2, T, T), lambda i: (i // 4, 0, i % 4, 0, 0)),
        ],
        out_specs=[out, out],
        out_shape=[jax.ShapeDtypeStruct((W, 2048), BF16)] * 2,
        compiler_params=params(),
        name="solve_cols",
    )(*inverse, x)


def solve_rows_kernel(meta, ihi, ilo, x_ref, ohi, olo, pan, y_ref):
    x = jnp.concatenate(
        [jnp.concatenate([x_ref[q, a] for q in range(8)], axis=1) for a in range(2)], axis=0
    )
    xs = split(x)
    for k in range(W // B):
        n = (k + 1) * B
        rows = slice(k * B, n)
        y_ref[:, rows] = dot3((xs[0][:, :n], xs[1][:, :n]), (ihi[rows, :n], ilo[rows, :n]), NT)
    at = pl.multiple_of(meta[COL_AT] * T, T)
    for a in range(2):
        pan[a] = y_ref[a * T : (a + 1) * T, pl.ds(at, T)]
    row = meta[ROW_AT]
    limit = jnp.where(row < 4, 0, jnp.where(row < 8, 512, W))
    limit = jnp.where(pl.program_id(0) == 0, limit, W)
    inside = lax.broadcasted_iota(jnp.int32, (T, W), 1) < limit
    y_ref[:T, :] = jnp.where(inside, y_ref[:T, :], F32(0))
    ohi[...], olo[...] = split(y_ref[...])


def solve_rows(meta, inverse, x):
    whole = pl.BlockSpec((W, W), lambda i, m: (0, 0))
    out = pl.BlockSpec((B, W), lambda i, m: (i, 0))
    return pl.pallas_call(
        solve_rows_kernel,
        grid_spec=pltpu.PrefetchScalarGridSpec(
            num_scalar_prefetch=1,
            grid=(4,),
            in_specs=[
                whole,
                whole,
                pl.BlockSpec((8, 2, T, T), lambda i, m: (0, i, 0, 0)),
            ],
            out_specs=[out, out, pl.BlockSpec((2, T, T), lambda i, m: (i, 0, 0))],
            scratch_shapes=[pltpu.VMEM((B, W), F32)],
        ),
        out_shape=[jax.ShapeDtypeStruct((W, W), BF16)] * 2 + [jax.ShapeDtypeStruct((8, T, T), F32)],
        compiler_params=params(),
        name="solve_rows",
    )(meta, *inverse, x)


def finish_kernel(meta, front, lhi, llo, chi, clo, pan, *rest):
    tiles, (out, p_ref) = rest[:-2], rest[-2:]
    for n in range(0, 2048, 512):
        cols = slice(n, n + 512)
        p_ref[:, cols] = dot3((lhi[...], llo[...]), (chi[:, cols], clo[:, cols]))
    flat_in = front.reshape(2 * T * 16, T)
    flat = out.reshape(2 * T * 16, T)
    for a in range(2):
        for lc in range(16):
            at = ((lc % 2) * 8 + lc // 2) * T
            where = pl.ds(a * T * 16 + lc, T, stride=16)
            flat[where, :] = flat_in[where, :] - p_ref[a * T : (a + 1) * T, at : at + T]
        row_tile = 2 * pl.program_id(0) + a
        for h in range(2):
            _, found = level_of(meta, h, row_tile)

            @pl.when(found == 1)
            def _():
                for kb in range(4):
                    got = tiles[(a * 2 + h) * 4 + kb]
                    for i in range(2):
                        where = pl.ds(a * T * 16 + local_col(meta, h, kb, i), T, stride=16)
                        flat[where, :] = flat[where, :] + got[i]

        kept = (row_tile == 0) & (meta[ROW_AT] < 4) & (meta[COL_AT] >= 4)

        @pl.when(jnp.logical_not(kept))
        def _():
            flat[pl.ds(a * T * 16, T, stride=16), :] = pan[a]


def finish(meta, front, rows, cols, pan, landed):
    def tile_spec(a, h, kb):
        return pl.BlockSpec(
            (None, None, None, 2, T, T),
            lambda i, m: (source_col(m, h, kb), h, level_of(m, h, 2 * i + a)[0], 0, 0, 0),
        )

    whole = pl.BlockSpec((W, 2048), lambda i, m: (0, 0))
    lhs = pl.BlockSpec((B, W), lambda i, m: (i, 0))
    block = pl.BlockSpec((2, T, 16, T), lambda i, m: (i, 0, 0, 0))
    specs = [tile_spec(a, h, kb) for a in range(2) for h in range(2) for kb in range(4)]
    return pl.pallas_call(
        finish_kernel,
        grid_spec=pltpu.PrefetchScalarGridSpec(
            num_scalar_prefetch=1,
            grid=(4,),
            in_specs=[block, lhs, lhs, whole, whole, pl.BlockSpec((2, T, T), lambda i, m: (i, 0, 0))]
            + specs,
            out_specs=block,
            scratch_shapes=[pltpu.VMEM((B, 2048), F32)],
        ),
        out_shape=jax.ShapeDtypeStruct(front.shape, F32),
        compiler_params=params(),
        name="finish",
    )(meta, front, *rows, *cols, pan, *([landed] * 16))


def spread(x, axis, n):
    copies = jnp.broadcast_to(x[None], (n,) + x.shape)
    return lax.all_to_all(copies, axis, split_axis=0, concat_axis=0, tiled=True)


def exchange(x, axis):
    return lax.all_to_all(x, axis, split_axis=0, concat_axis=0, tiled=True)


def shards(front, child_blocks, child_map):
    row = lax.axis_index("row")
    col = lax.axis_index("col")
    meta = jnp.concatenate([child_map.reshape(-1), jnp.stack([row, col])]).astype(jnp.int32)
    lower_half = row < 8

    arrived = exchange(pack_rows(meta, child_blocks), "row")
    got = exchange(pack_cols(meta, arrived, 1), "col")
    first = first_row(meta, front, got)

    down = [(i, i + 8) for i in range(8)]
    ours = jnp.where(lower_half, first[:8], lax.ppermute(first[8:], "row", down))
    pivot = jnp.where(lower_half, first[0, :64], lax.ppermute(first[0, 64:], "row", down))

    pivots = spread(spread(pivot, "col", 8), "row", 16)
    inverse = invert(pivots)

    cols_x = lax.all_gather(ours, "row").reshape(2, 8, 8, T, T)
    turn = [
        ((q + 8 * t) * 8 + c, (c + 8 * t) * 8 + q)
        for t in range(2)
        for q in range(8)
        for c in range(8)
    ]
    turned = lax.ppermute(jnp.swapaxes(ours, 1, 2), ("row", "col"), turn)
    rows_x = lax.all_gather(turned, "col")

    landed = exchange(pack_cols(meta, arrived, 4), "col")

    cols_l = solve_cols(inverse, cols_x)
    *rows_l, pan = solve_rows(meta, inverse, rows_x)
    return finish(meta, front, rows_l, cols_l, pan, landed)


def solution(mesh):
    in_specs = (P(None, "row", None, "col"), P(None, None, "row", None, "col"), P())
    out_specs = P(None, "row", None, "col")
    return jax.shard_map(shards, mesh=mesh, in_specs=in_specs, out_specs=out_specs, check_vma=False)
```

```python
import functools

import jax
import jax.numpy as jnp
from jax import lax
from jax.experimental import pallas as pl
from jax.experimental.pallas import tpu as pltpu
from jax.sharding import PartitionSpec as P

T = 128
W = 1024
F32 = jnp.float32
BF16 = jnp.bfloat16
HIGHEST = lax.Precision.HIGHEST
ROW_AT = 128
COL_AT = 129
VMEM = 58 * 1024 * 1024


def params(**kw):
    return pltpu.CompilerParams(vmem_limit_bytes=VMEM, **kw)


def shift(meta, h, k):
    return meta[h * 64 + 16 * k] & 15


def source_row(meta, h, ka):
    return (meta[ROW_AT] - shift(meta, h, ka)) & 15


def local_row(meta, h, ka):
    return meta[h * 64 + source_row(meta, h, ka) + 16 * ka] >> 4


def level_of(meta, h, a):
    ka = jnp.int32(0)
    found = jnp.int32(0)
    for k in range(4):
        hit = local_row(meta, h, k) == a
        ka = jnp.where(hit, k, ka)
        found = jnp.where(hit, 1, found)
    return ka, found


def dest_col(meta, h, kb):
    return (meta[COL_AT] + shift(meta, h, kb)) & 7


def source_col(meta, h, kb):
    return (meta[COL_AT] - shift(meta, h, kb)) & 7


def local_col(meta, h, kb, i):
    return meta[h * 64 + source_col(meta, h, kb) + 8 * (2 * kb + i)] >> 3


def split(x):
    hi = x.astype(BF16)
    return hi, (x - hi.astype(F32)).astype(BF16)


def dot(a, b, dims=((1,), (0,)), precision=None):
    return lax.dot_general(a, b, (dims, ((), ())), precision=precision, preferred_element_type=F32)


NT = ((1,), (1,))


def dot3(a, b, dims=((1,), (0,))):
    return dot(a[0], b[0], dims) + (dot(a[0], b[1], dims) + dot(a[1], b[0], dims))


def pack_rows_kernel(meta, child_ref, out_ref):
    flat = child_ref.reshape(T * 8, T)
    for j in range(8):
        out_ref[0, j] = flat[pl.ds(j, T, stride=8), :]


def pack_rows(meta, child):
    return pl.pallas_call(
        pack_rows_kernel,
        grid_spec=pltpu.PrefetchScalarGridSpec(
            num_scalar_prefetch=1,
            grid=(2, 4),
            in_specs=[pl.BlockSpec((None, None, T, 8, T), lambda h, k, m: (h, k, 0, 0, 0))],
            out_specs=pl.BlockSpec(
                (1, 8, T, T), lambda h, k, m: ((m[ROW_AT] + shift(m, h, k)) & 15, 0, 0, 0)
            ),
        ),
        out_shape=jax.ShapeDtypeStruct((16, 8, T, T), F32),
        compiler_params=params(),
        name="pack_rows",
    )(meta, child)


def pack_cols_kernel(meta, *refs):
    for lev in range(4):
        refs[4][lev] = refs[lev][...]


def pack_cols(meta, arrived):
    def source(lev):
        return pl.BlockSpec((None, 2, T, T), lambda h, kb, m: (source_row(m, h, lev), kb, 0, 0))

    return pl.pallas_call(
        pack_cols_kernel,
        grid_spec=pltpu.PrefetchScalarGridSpec(
            num_scalar_prefetch=1,
            grid=(2, 4),
            in_specs=[source(lev) for lev in range(4)],
            out_specs=pl.BlockSpec(
                (None, None, 4, 2, T, T), lambda h, kb, m: (dest_col(m, h, kb), h, 0, 0, 0, 0)
            ),
        ),
        out_shape=jax.ShapeDtypeStruct((8, 2, 4, 2, T, T), F32),
        compiler_params=params(),
        name="pack_cols",
    )(meta, *([arrived] * 4))


def place(lc):
    return (lc & 1) * 8 + (lc >> 1)


def assemble_kernel(start, meta, front_ref, *refs):
    tiles, out_ref = refs[:-1], refs[-1]
    flat = front_ref.reshape(T * 16, T)
    for lc in range(16):
        out_ref[place(lc)] = flat[pl.ds(lc, T, stride=16), :]
    for h in range(2):
        _, found = level_of(meta, h, start + pl.program_id(0))

        @pl.when(found == 1)
        def _():
            for kb in range(4):
                for i in range(2):
                    at = place(local_col(meta, h, kb, i))
                    out_ref[at] = out_ref[at] + tiles[4 * h + kb][i]


def assemble(meta, front, landed, start, count):
    def tile_spec(h, kb):
        return pl.BlockSpec(
            (None, None, None, 2, T, T),
            lambda i, m: (source_col(m, h, kb), h, level_of(m, h, start + i)[0], 0, 0, 0),
        )

    return pl.pallas_call(
        functools.partial(assemble_kernel, start),
        grid_spec=pltpu.PrefetchScalarGridSpec(
            num_scalar_prefetch=1,
            grid=(count,),
            in_specs=[pl.BlockSpec((None, T, 16, T), lambda i, m: (start + i, 0, 0, 0))]
            + [tile_spec(h, kb) for h in range(2) for kb in range(4)],
            out_specs=pl.BlockSpec((None, 16, T, T), lambda i, m: (i, 0, 0, 0)),
        ),
        out_shape=jax.ShapeDtypeStruct((count, 16, T, T), F32),
        compiler_params=params(),
        cost_estimate=pl.CostEstimate(flops=0, bytes_accessed=count * 5 << 19, transcendentals=0),
        name=f"assemble_{count}",
    )(meta, front, *([landed] * 8))


def root(x):
    r = lax.rsqrt(x)
    return r * (1.5 - 0.5 * x * r * r)


def inverse_of(x):
    r = pl.reciprocal(x, approx=True)
    r = r * (2.0 - x * r)
    return r * (2.0 - x * r)


def invert_kernel(meta, own, other, hi_ref, lo_ref, a_ref, t_ref, l_ref):
    row, col = meta[ROW_AT], meta[COL_AT]
    for q in range(8):
        same = ((row ^ q) & 1) == 0
        dz = ((row >> 1) - (q >> 1)) & 3
        for c in range(8):
            at = (dz, ((col >> 1) - (c >> 1)) & 3, (col ^ c) & 1)
            a_ref[q * T : (q + 1) * T, c * T : (c + 1) * T] = jnp.where(same, own[at], other[at])
    t_ref[...] = jnp.zeros_like(t_ref)
    sub = lax.broadcasted_iota(jnp.int32, (8, T), 0)
    lane = lax.broadcasted_iota(jnp.int32, (8, T), 1)

    def over(x):
        return jnp.broadcast_to(x, (8, T))

    def step(k, _):
        at = pl.multiple_of(k * T, T)
        s = [a_ref[pl.ds(at + 8 * b, 8), pl.ds(at, T)] for b in range(16)]
        on_diagonal = [lane == sub + 8 * b for b in range(16)]
        only = [jnp.where(on_diagonal[b], s[b], F32(0)) for b in range(16)]
        total = only[0]
        for b in range(1, 16):
            total = total + only[b]
        by_lane = over(root(jnp.sum(total, axis=0, keepdims=True)))
        s = [s[b] * (over(root(jnp.sum(only[b], axis=1, keepdims=True))) * by_lane) for b in range(16)]
        t = [jnp.where(on_diagonal[b], F32(1), F32(0)) for b in range(16)]
        for j in range(0, T, 4):
            b0, i0 = divmod(j, 8)
            p = [[over(s[b0][i0 + i : i0 + i + 1, j + c : j + c + 1]) for c in range(i + 1)] for i in range(4)]
            sr = [over(s[b0][i0 + i : i0 + i + 1, :]) for i in range(4)]
            tr = [over(t[b0][i0 + i : i0 + i + 1, :]) for i in range(4)]
            (p00,), (p10, p11), (p20, p21, p22), (p30, p31, p32, p33) = p
            first = inverse_of(p00 * p11 - p10 * p10)
            x20 = (p20 * p11 - p21 * p10) * first
            x21 = (p21 * p00 - p20 * p10) * first
            x30 = (p30 * p11 - p31 * p10) * first
            x31 = (p31 * p00 - p30 * p10) * first
            s22 = p22 - (x20 * p20 + x21 * p21)
            s32 = p32 - (x30 * p20 + x31 * p21)
            s33 = p33 - (x30 * p30 + x31 * p31)
            second = inverse_of(s22 * s33 - s32 * s32)
            y00, y10, y11 = p11 * first, p10 * first, p00 * first
            y22, y32, y33 = s33 * second, s32 * second, s22 * second

            def solved(rows):
                r2 = rows[2] - (x20 * rows[0] + x21 * rows[1])
                r3 = rows[3] - (x30 * rows[0] + x31 * rows[1])
                z2 = y22 * r2 - y32 * r3
                z3 = y33 * r3 - y32 * r2
                z0 = (y00 * rows[0] - y10 * rows[1]) - (x20 * z2 + x30 * z3)
                z1 = (y11 * rows[1] - y10 * rows[0]) - (x21 * z2 + x31 * z3)
                return (z0, z1, z2, z3), r2, r3

            zs, _, _ = solved(sr)
            zt, t2, t3 = solved(tr)
            r0 = root(p00)
            l10 = p10 * r0
            r1 = root(p11 - l10 * l10)
            r2 = root(s22)
            l32 = s32 * r2
            r3 = root(s33 - l32 * l32)
            done = (
                tr[0] * r0,
                (tr[1] - l10 * r0 * tr[0]) * r1,
                t2 * r2,
                (t3 - l32 * r2 * t2) * r3,
            )
            for b in range(b0 if i0 == 0 else b0 + 1, 16):
                v = [over(s[b][:, j + c : j + c + 1]) for c in range(4)]
                if b == b0:
                    v = [jnp.where(sub > 3, x, F32(0)) for x in v]
                s[b] = s[b] - ((v[0] * zs[0] + v[1] * zs[1]) + (v[2] * zs[2] + v[3] * zs[3]))
                t[b] = t[b] - ((v[0] * zt[0] + v[1] * zt[1]) + (v[2] * zt[2] + v[3] * zt[3]))
            for i in range(4):
                t[b0] = jnp.where(sub == i0 + i, done[i], t[b0])
        t = [x * by_lane for x in t]
        kinv = jnp.concatenate(t, axis=0)
        for kk in range(8):

            @pl.when(k == kk)
            def _():
                lo, hi = kk * T, (kk + 1) * T
                if kk:
                    t_ref[lo:hi, :lo] = dot(kinv, t_ref[lo:hi, :lo], precision=HIGHEST)
                t_ref[lo:hi, lo:hi] = kinv
                if kk < 7:
                    col = dot(a_ref[hi:, lo:hi], kinv, NT, precision=HIGHEST)
                    l_ref[hi:, :] = col
                    for n0 in range(hi, W, T):
                        a_ref[n0:, n0 : n0 + T] = a_ref[n0:, n0 : n0 + T] - dot(
                            l_ref[n0:, :], l_ref[n0 : n0 + T, :], NT, precision=HIGHEST
                        )
                    t_ref[hi:, :hi] = t_ref[hi:, :hi] - dot(
                        l_ref[hi:, :], t_ref[lo:hi, :hi], precision=HIGHEST
                    )

        return 0

    lax.fori_loop(0, 8, step, 0)
    hi_ref[...], lo_ref[...] = split(t_ref[...])


def invert(meta, own, other):
    whole = pl.BlockSpec(memory_space=pltpu.VMEM)
    return pl.pallas_call(
        invert_kernel,
        in_specs=[pl.BlockSpec(memory_space=pltpu.SMEM), whole, whole],
        out_specs=[whole, whole],
        out_shape=[jax.ShapeDtypeStruct((W, W), BF16)] * 2,
        scratch_shapes=[
            pltpu.VMEM((W, W), F32),
            pltpu.VMEM((W, W), F32),
            pltpu.VMEM((W, T), F32),
        ],
        compiler_params=params(),
        cost_estimate=pl.CostEstimate(flops=80_000_000_000, bytes_accessed=8 << 20, transcendentals=0),
        name="invert",
    )(meta, own, other)


B = 256


def solve_cols_kernel(ihi, ilo, x_ref, ohi, olo, y_ref):
    for k in range(W // B):
        x = jnp.concatenate(
            [jnp.concatenate([x_ref[q, 0], x_ref[q, 1]], axis=1) for q in (2 * k, 2 * k + 1)], axis=0
        )
        cols = slice(k * B, (k + 1) * B)
        y = dot3((ihi[k * B :, cols], ilo[k * B :, cols]), split(x))
        y_ref[k * B :, :] = y if k == 0 else y_ref[k * B :, :] + y
        ohi[cols, :], olo[cols, :] = split(y_ref[cols, :])


def solve_cols(inverse, x):
    whole = pl.BlockSpec((W, W), lambda i: (0, 0))
    out = pl.BlockSpec((W, B), lambda i: (0, i))
    return pl.pallas_call(
        solve_cols_kernel,
        grid=(8,),
        in_specs=[
            whole,
            whole,
            pl.BlockSpec((None, 8, 2, T, T), lambda i: (i // 4, 0, i % 4, 0, 0)),
        ],
        out_specs=[out, out],
        out_shape=[jax.ShapeDtypeStruct((W, 2048), BF16)] * 2,
        scratch_shapes=[pltpu.VMEM((W, B), F32)],
        compiler_params=params(),
        name="solve_cols",
    )(*inverse, x)


H = 4


def solve_rows_kernel(meta, ihi, ilo, *refs):
    xs, (ohi, olo, pan, xhi, xlo, y_ref) = refs[:4], refs[4:]
    for d in range(8):
        q = (((meta[COL_AT] >> 1) - (d >> 1)) & 3) * 2 + ((meta[COL_AT] ^ d) & 1)
        cols = pl.ds(pl.multiple_of(q * T, T), T)
        for a in range(H):
            rows = slice(a * T, (a + 1) * T)
            xhi[rows, cols], xlo[rows, cols] = split(xs[d >> 1][d & 1, a])
    for k in range(W // B):
        n = (k + 1) * B
        rows = slice(k * B, n)
        y_ref[:, rows] = dot3((xhi[:, :n], xlo[:, :n]), (ihi[rows, :n], ilo[rows, :n]), NT)
    at = pl.multiple_of(meta[COL_AT] * T, T)
    for a in range(H):
        pan[a] = y_ref[a * T : (a + 1) * T, pl.ds(at, T)]
    row = meta[ROW_AT]
    limit = jnp.where(row < 4, 0, jnp.where(row < 8, 512, W))
    limit = jnp.where(pl.program_id(0) == 0, limit, W)
    inside = lax.broadcasted_iota(jnp.int32, (T, W), 1) < limit
    y_ref[:T, :] = jnp.where(inside, y_ref[:T, :], F32(0))
    ohi[...], olo[...] = split(y_ref[...])


def solve_rows(meta, inverse, xs):
    whole = pl.BlockSpec((W, W), lambda i, m: (0, 0))
    out = pl.BlockSpec((H * T, W), lambda i, m: (i, 0))
    tiles = pl.BlockSpec((H, T, T), lambda i, m: (i, 0, 0))
    return pl.pallas_call(
        solve_rows_kernel,
        grid_spec=pltpu.PrefetchScalarGridSpec(
            num_scalar_prefetch=1,
            grid=(8 // H,),
            in_specs=[whole, whole] + [pl.BlockSpec((2, H, T, T), lambda i, m: (0, i, 0, 0))] * 4,
            out_specs=[out, out, tiles],
            scratch_shapes=[
                pltpu.VMEM((H * T, W), BF16),
                pltpu.VMEM((H * T, W), BF16),
                pltpu.VMEM((H * T, W), F32),
            ],
        ),
        out_shape=[jax.ShapeDtypeStruct((W, W), BF16)] * 2 + [jax.ShapeDtypeStruct((8, T, T), F32)],
        compiler_params=params(),
        name="solve_rows",
    )(meta, *inverse, *xs)


F = 2


def finish_kernel(meta, m_ref, lhi, llo, chi, clo, pan, out):
    flat = out.reshape(F * T * 16, T)
    for n in range(0, 2048, 512):
        cols = slice(n, n + 512)
        p = dot3((lhi[...], llo[...]), (chi[:, cols], clo[:, cols]))
        for a in range(F):
            for at in range(n // T, n // T + 4):
                lc = (at % 8) * 2 + at // 8
                flat[pl.ds(a * T * 16 + lc, T, stride=16), :] = (
                    m_ref[a, at] - p[a * T : (a + 1) * T, (at * T) % 512 : (at * T) % 512 + T]
                )
    for a in range(F):
        kept = (pl.program_id(0) * F + a == 0) & (meta[ROW_AT] < 4) & (meta[COL_AT] >= 4)

        @pl.when(jnp.logical_not(kept))
        def _():
            flat[pl.ds(a * T * 16, T, stride=16), :] = pan[a]


def finish(meta, m, rows, cols, pan):
    whole = pl.BlockSpec((W, 2048), lambda i, m: (0, 0))
    lhs = pl.BlockSpec((F * T, W), lambda i, m: (i, 0))
    return pl.pallas_call(
        finish_kernel,
        grid_spec=pltpu.PrefetchScalarGridSpec(
            num_scalar_prefetch=1,
            grid=(8 // F,),
            in_specs=[
                pl.BlockSpec((F, 16, T, T), lambda i, m: (i, 0, 0, 0)),
                lhs,
                lhs,
                whole,
                whole,
                pl.BlockSpec((F, T, T), lambda i, m: (i, 0, 0)),
            ],
            out_specs=pl.BlockSpec((F, T, 16, T), lambda i, m: (i, 0, 0, 0)),
        ),
        out_shape=jax.ShapeDtypeStruct((8, T, 16, T), F32),
        compiler_params=params(),
        name="finish",
    )(meta, m, *rows, *cols, pan)


def exchange(x, axis):
    return lax.all_to_all(x, axis, split_axis=0, concat_axis=0, tiled=True)


def row_id(y, z, core):
    return (y % 2) * 8 + (z % 4) * 2 + core % 2


def col_id(x, y):
    return (x % 4) * 2 + y % 2


def along_row(v, dy, dz, dcore):
    pairs = [
        (row_id(y, z, core), row_id(y + dy, z + dz, core + dcore))
        for y in range(2)
        for z in range(4)
        for core in range(2)
    ]
    return lax.ppermute(v, "row", pairs)


def along_col(v, dx, dy):
    return lax.ppermute(
        v, "col", [(col_id(x, y), col_id(x + dx, y + dy)) for x in range(4) for y in range(2)]
    )


def down(v):
    return lax.ppermute(v, "row", [(i, i + 8) for i in range(8)])


def shards(front, child_blocks, child_map):
    row = lax.axis_index("row")
    col = lax.axis_index("col")
    meta = jnp.concatenate([child_map.reshape(-1), jnp.stack([row, col])]).astype(jnp.int32)
    upper = row < 8

    arrived = exchange(pack_rows(meta, child_blocks), "row")
    landed = exchange(pack_cols(meta, arrived), "col")
    first = assemble(meta, front, landed, 0, 1)[0]

    tile = jnp.where(upper, first[0], down(first[0]))
    two = jnp.stack([tile, along_col(tile, 0, 1)])
    two, first = lax.optimization_barrier((two, first))
    line = jnp.stack([two] + [along_col(two, dx, 0) for dx in (1, 2, 3)])
    ours = jnp.where(upper, first[:8], down(first[8:]))
    line, landed, front = lax.optimization_barrier((line, landed, front))
    parts = [line] + [along_row(line, 0, dz, 0) for dz in (1, 2, 3)]
    matrix = assemble(meta, front, landed, 0, 8)
    parts, matrix, ours = lax.optimization_barrier((parts, matrix, ours))
    own = jnp.stack(parts)
    other = along_row(own, 0, 0, 1)

    mine = matrix[:, 0]
    pair = jnp.stack([mine, along_col(mine, 0, 1)])
    cols_x = lax.all_gather(ours, "row").reshape(2, 8, 8, T, T)
    other, pair = lax.optimization_barrier((other, pair))
    rows_x = [pair] + [along_col(pair, dx, 0) for dx in (1, 2, 3)]

    inverse = invert(meta, own, other)
    *rows_l, pan = solve_rows(meta, inverse, rows_x)
    cols_l = solve_cols(inverse, cols_x)
    return finish(meta, matrix, rows_l, cols_l, pan)


def solution(mesh):
    in_specs = (P(None, "row", None, "col"), P(None, None, "row", None, "col"), P())
    out_specs = P(None, "row", None, "col")
    return jax.shard_map(shards, mesh=mesh, in_specs=in_specs, out_specs=out_specs, check_vma=False)
```

```python
import functools

import jax
import jax.numpy as jnp
from jax import lax
from jax.experimental import pallas as pl
from jax.experimental.pallas import tpu as pltpu
from jax.sharding import PartitionSpec as P

T = 128
W = 1024
F32 = jnp.float32
BF16 = jnp.bfloat16
HIGHEST = lax.Precision.HIGHEST
ROW_AT = 128
COL_AT = 129
VMEM = 58 * 1024 * 1024


def params(**kw):
    return pltpu.CompilerParams(vmem_limit_bytes=VMEM, **kw)


def shift(meta, h, k):
    return meta[h * 64 + 16 * k] & 15


def source_row(meta, h, ka):
    return (meta[ROW_AT] - shift(meta, h, ka)) & 15


def local_row(meta, h, ka):
    return meta[h * 64 + source_row(meta, h, ka) + 16 * ka] >> 4


def level_of(meta, h, a):
    ka = jnp.int32(0)
    found = jnp.int32(0)
    for k in range(4):
        hit = local_row(meta, h, k) == a
        ka = jnp.where(hit, k, ka)
        found = jnp.where(hit, 1, found)
    return ka, found


def dest_col(meta, h, kb):
    return (meta[COL_AT] + shift(meta, h, kb)) & 7


def source_col(meta, h, kb):
    return (meta[COL_AT] - shift(meta, h, kb)) & 7


def local_col(meta, h, kb, i):
    return meta[h * 64 + source_col(meta, h, kb) + 8 * (2 * kb + i)] >> 3


def split(x):
    hi = x.astype(BF16)
    return hi, (x - hi.astype(F32)).astype(BF16)


def dot(a, b, dims=((1,), (0,)), precision=None):
    return lax.dot_general(a, b, (dims, ((), ())), precision=precision, preferred_element_type=F32)


NT = ((1,), (1,))


def dot3(a, b, dims=((1,), (0,))):
    return dot(a[0], b[0], dims) + (dot(a[0], b[1], dims) + dot(a[1], b[0], dims))


def pack_rows_kernel(meta, child_ref, out_ref):
    flat = child_ref.reshape(T * 8, T)
    for j in range(8):
        out_ref[0, j] = flat[pl.ds(j, T, stride=8), :]


def pack_rows(meta, child):
    return pl.pallas_call(
        pack_rows_kernel,
        grid_spec=pltpu.PrefetchScalarGridSpec(
            num_scalar_prefetch=1,
            grid=(2, 4),
            in_specs=[pl.BlockSpec((None, None, T, 8, T), lambda h, k, m: (h, k, 0, 0, 0))],
            out_specs=pl.BlockSpec(
                (1, 8, T, T), lambda h, k, m: ((m[ROW_AT] + shift(m, h, k)) & 15, 0, 0, 0)
            ),
        ),
        out_shape=jax.ShapeDtypeStruct((16, 8, T, T), F32),
        compiler_params=params(),
        name="pack_rows",
    )(meta, child)


def pack_cols_kernel(meta, *refs):
    for lev in range(4):
        refs[4][lev] = refs[lev][...]


def pack_cols(meta, arrived):
    def source(lev):
        return pl.BlockSpec((None, 2, T, T), lambda h, kb, m: (source_row(m, h, lev), kb, 0, 0))

    return pl.pallas_call(
        pack_cols_kernel,
        grid_spec=pltpu.PrefetchScalarGridSpec(
            num_scalar_prefetch=1,
            grid=(2, 4),
            in_specs=[source(lev) for lev in range(4)],
            out_specs=pl.BlockSpec(
                (None, None, 4, 2, T, T), lambda h, kb, m: (dest_col(m, h, kb), h, 0, 0, 0, 0)
            ),
        ),
        out_shape=jax.ShapeDtypeStruct((8, 2, 4, 2, T, T), F32),
        compiler_params=params(),
        name="pack_cols",
    )(meta, *([arrived] * 4))


def place(lc):
    return (lc & 1) * 8 + (lc >> 1)


def assemble_kernel(start, meta, front_ref, *refs):
    tiles, out_ref = refs[:-1], refs[-1]
    flat = front_ref.reshape(T * 16, T)
    for lc in range(16):
        out_ref[place(lc)] = flat[pl.ds(lc, T, stride=16), :]
    for h in range(2):
        _, found = level_of(meta, h, start + pl.program_id(0))

        @pl.when(found == 1)
        def _():
            for kb in range(4):
                for i in range(2):
                    at = place(local_col(meta, h, kb, i))
                    out_ref[at] = out_ref[at] + tiles[4 * h + kb][i]


def assemble(meta, front, landed, start, count):
    def tile_spec(h, kb):
        return pl.BlockSpec(
            (None, None, None, 2, T, T),
            lambda i, m: (source_col(m, h, kb), h, level_of(m, h, start + i)[0], 0, 0, 0),
        )

    return pl.pallas_call(
        functools.partial(assemble_kernel, start),
        grid_spec=pltpu.PrefetchScalarGridSpec(
            num_scalar_prefetch=1,
            grid=(count,),
            in_specs=[pl.BlockSpec((None, T, 16, T), lambda i, m: (start + i, 0, 0, 0))]
            + [tile_spec(h, kb) for h in range(2) for kb in range(4)],
            out_specs=pl.BlockSpec((None, 16, T, T), lambda i, m: (i, 0, 0, 0)),
        ),
        out_shape=jax.ShapeDtypeStruct((count, 16, T, T), F32),
        compiler_params=params(),
        cost_estimate=pl.CostEstimate(flops=0, bytes_accessed=count * 5 << 19, transcendentals=0),
        name=f"assemble_{count}",
    )(meta, front, *([landed] * 8))


def tile_of_first_col(meta, h):
    at = jnp.int32(0)
    found = jnp.int32(0)
    for kb in range(4):
        for i in range(2):
            hit = local_col(meta, h, kb, i) == 0
            at = jnp.where(hit, 2 * kb + i, at)
            found = jnp.where(hit, 1, found)
    return at >> 1, at & 1, found


def first_col_kernel(meta, front_ref, *refs):
    tiles, out_ref = refs[:-1], refs[-1]
    flat = front_ref.reshape(8 * T * 8, T)
    for a in range(8):
        out_ref[a] = flat[pl.ds(a * T * 8, T, stride=8), :]
    for h in range(2):
        _, _, found = tile_of_first_col(meta, h)

        @pl.when(found == 1)
        def _():
            for ka in range(4):
                a = local_row(meta, h, ka)
                out_ref[a] = out_ref[a] + tiles[4 * h + ka][...]


def first_col(meta, front, landed):
    def tile_spec(h, ka):
        def at(i, m):
            kb, j, _ = tile_of_first_col(m, h)
            return source_col(m, h, kb), h, ka, j, 0, 0

        return pl.BlockSpec((None, None, None, None, T, T), at)

    whole = pl.BlockSpec((8, T, T), lambda i, m: (0, 0, 0))
    return pl.pallas_call(
        first_col_kernel,
        grid_spec=pltpu.PrefetchScalarGridSpec(
            num_scalar_prefetch=1,
            grid=(1,),
            in_specs=[pl.BlockSpec((8, T, 8, T), lambda i, m: (0, 0, 0, 0))]
            + [tile_spec(h, ka) for h in range(2) for ka in range(4)],
            out_specs=whole,
        ),
        out_shape=jax.ShapeDtypeStruct((8, T, T), F32),
        compiler_params=params(),
        name="first_col",
    )(meta, front, *([landed] * 8))


def root(x):
    r = lax.rsqrt(x)
    return r * (1.5 - 0.5 * x * r * r)


def inverse_of(x):
    return pl.reciprocal(x, approx=False)


def invert_kernel(meta, own, other, hi_ref, lo_ref, a_ref, t_ref, l_ref):
    row, col = meta[ROW_AT], meta[COL_AT]
    for q in range(8):
        same = ((row ^ q) & 1) == 0
        dz = ((row >> 1) - (q >> 1)) & 3
        for c in range(8):
            at = (dz, ((col >> 1) - (c >> 1)) & 3, (col ^ c) & 1)
            a_ref[q * T : (q + 1) * T, c * T : (c + 1) * T] = jnp.where(same, own[at], other[at])
    t_ref[...] = jnp.zeros_like(t_ref)
    sub = lax.broadcasted_iota(jnp.int32, (8, T), 0)
    lane = lax.broadcasted_iota(jnp.int32, (8, T), 1)

    def over(x):
        return jnp.broadcast_to(x, (8, T))

    def step(k, _):
        at = pl.multiple_of(k * T, T)
        s = [a_ref[pl.ds(at + 8 * b, 8), pl.ds(at, T)] for b in range(16)]
        on_diagonal = [lane == sub + 8 * b for b in range(16)]
        only = [jnp.where(on_diagonal[b], s[b], F32(0)) for b in range(16)]
        total = only[0]
        for b in range(1, 16):
            total = total + only[b]
        by_lane = over(root(jnp.sum(total, axis=0, keepdims=True)))
        s = [s[b] * (over(root(jnp.sum(only[b], axis=1, keepdims=True))) * by_lane) for b in range(16)]
        t = [jnp.where(on_diagonal[b], F32(1), F32(0)) for b in range(16)]
        for j in range(0, T, 4):
            b0, i0 = divmod(j, 8)
            p = [[over(s[b0][i0 + i : i0 + i + 1, j + c : j + c + 1]) for c in range(i + 1)] for i in range(4)]
            sr = [over(s[b0][i0 + i : i0 + i + 1, :]) for i in range(4)]
            tr = [over(t[b0][i0 + i : i0 + i + 1, :]) for i in range(4)]
            (p00,), (p10, p11), (p20, p21, p22), (p30, p31, p32, p33) = p
            first = inverse_of(p00 * p11 - p10 * p10)
            x20 = (p20 * p11 - p21 * p10) * first
            x21 = (p21 * p00 - p20 * p10) * first
            x30 = (p30 * p11 - p31 * p10) * first
            x31 = (p31 * p00 - p30 * p10) * first
            s22 = p22 - (x20 * p20 + x21 * p21)
            s32 = p32 - (x30 * p20 + x31 * p21)
            s33 = p33 - (x30 * p30 + x31 * p31)
            second = inverse_of(s22 * s33 - s32 * s32)
            y00, y10, y11 = p11 * first, p10 * first, p00 * first
            y22, y32, y33 = s33 * second, s32 * second, s22 * second

            def solved(rows):
                r2 = rows[2] - (x20 * rows[0] + x21 * rows[1])
                r3 = rows[3] - (x30 * rows[0] + x31 * rows[1])
                z2 = y22 * r2 - y32 * r3
                z3 = y33 * r3 - y32 * r2
                z0 = (y00 * rows[0] - y10 * rows[1]) - (x20 * z2 + x30 * z3)
                z1 = (y11 * rows[1] - y10 * rows[0]) - (x21 * z2 + x31 * z3)
                return (z0, z1, z2, z3), r2, r3

            zs, _, _ = solved(sr)
            zt, t2, t3 = solved(tr)
            r0 = root(p00)
            l10 = p10 * r0
            r1 = root(p11 - l10 * l10)
            r2 = root(s22)
            l32 = s32 * r2
            r3 = root(s33 - l32 * l32)
            done = (
                tr[0] * r0,
                (tr[1] - l10 * r0 * tr[0]) * r1,
                t2 * r2,
                (t3 - l32 * r2 * t2) * r3,
            )
            for b in range(b0 if i0 == 0 else b0 + 1, 16):
                v = [over(s[b][:, j + c : j + c + 1]) for c in range(4)]
                if b == b0:
                    v = [jnp.where(sub > 3, x, F32(0)) for x in v]
                s[b] = s[b] - ((v[0] * zs[0] + v[1] * zs[1]) + (v[2] * zs[2] + v[3] * zs[3]))
                t[b] = t[b] - ((v[0] * zt[0] + v[1] * zt[1]) + (v[2] * zt[2] + v[3] * zt[3]))
            for i in range(4):
                t[b0] = jnp.where(sub == i0 + i, done[i], t[b0])
        t = [x * by_lane for x in t]
        kinv = jnp.concatenate(t, axis=0)
        for kk in range(8):

            @pl.when(k == kk)
            def _():
                lo, hi = kk * T, (kk + 1) * T
                if kk:
                    t_ref[lo:hi, :lo] = dot(kinv, t_ref[lo:hi, :lo], precision=HIGHEST)
                t_ref[lo:hi, lo:hi] = kinv
                if kk < 7:
                    col = dot(a_ref[hi:, lo:hi], kinv, NT, precision=HIGHEST)
                    l_ref[hi:, :] = col
                    for n0 in range(hi, W, T):
                        a_ref[n0:, n0 : n0 + T] = a_ref[n0:, n0 : n0 + T] - dot(
                            l_ref[n0:, :], l_ref[n0 : n0 + T, :], NT, precision=HIGHEST
                        )
                    t_ref[hi:, :hi] = t_ref[hi:, :hi] - dot(
                        l_ref[hi:, :], t_ref[lo:hi, :hi], precision=HIGHEST
                    )

        return 0

    lax.fori_loop(0, 8, step, 0)
    hi_ref[...], lo_ref[...] = split(t_ref[...])


def invert(meta, own, other):
    whole = pl.BlockSpec(memory_space=pltpu.VMEM)
    return pl.pallas_call(
        invert_kernel,
        in_specs=[pl.BlockSpec(memory_space=pltpu.SMEM), whole, whole],
        out_specs=[whole, whole],
        out_shape=[jax.ShapeDtypeStruct((W, W), BF16)] * 2,
        scratch_shapes=[
            pltpu.VMEM((W, W), F32),
            pltpu.VMEM((W, W), F32),
            pltpu.VMEM((W, T), F32),
        ],
        compiler_params=params(),
        cost_estimate=pl.CostEstimate(flops=80_000_000_000, bytes_accessed=8 << 20, transcendentals=0),
        name="invert",
    )(meta, own, other)


B = 256
H = 4
F = 2
ROW_STEPS = 8 // H
COL_STEPS = 2048 // B
END_STEPS = 8 // F


def rows_step(meta, i, inverse, xs, lhs, pan, x_refs, y_ref):
    ihi, ilo = inverse
    xhi, xlo = x_refs
    for d in range(8):
        q = (((meta[COL_AT] >> 1) - (d >> 1)) & 3) * 2 + ((meta[COL_AT] ^ d) & 1)
        cols = pl.ds(pl.multiple_of(q * T, T), T)
        for a in range(H):
            rows = slice(a * T, (a + 1) * T)
            xhi[rows, cols], xlo[rows, cols] = split(xs[d >> 1][d & 1, a])
    for k in range(W // B):
        n = (k + 1) * B
        rows = slice(k * B, n)
        y_ref[:, rows] = dot3((xhi[:, :n], xlo[:, :n]), (ihi[rows, :n], ilo[rows, :n]), NT)
    at = pl.multiple_of(meta[COL_AT] * T, T)
    for a in range(H):
        pan[i * H + a] = y_ref[a * T : (a + 1) * T, pl.ds(at, T)]
    row = meta[ROW_AT]
    limit = jnp.where(row < 4, 0, jnp.where(row < 8, 512, W))
    limit = jnp.where(i == 0, limit, W)
    inside = lax.broadcasted_iota(jnp.int32, (T, W), 1) < limit
    y_ref[:T, :] = jnp.where(inside, y_ref[:T, :], F32(0))
    where = pl.ds(pl.multiple_of(i * H * T, H * T), H * T)
    lhs[0][where, :], lhs[1][where, :] = split(y_ref[...])


def cols_step(i, inverse, x_ref, rhs, y_ref):
    ihi, ilo = inverse
    where = pl.ds(pl.multiple_of(i * B, B), B)
    for k in range(W // B):
        x = jnp.concatenate(
            [jnp.concatenate([x_ref[q, 0], x_ref[q, 1]], axis=1) for q in (2 * k, 2 * k + 1)], axis=0
        )
        cols = slice(k * B, (k + 1) * B)
        y = dot3((ihi[k * B :, cols], ilo[k * B :, cols]), split(x))
        y_ref[k * B :, :] = y if k == 0 else y_ref[k * B :, :] + y
        rhs[0][cols, where], rhs[1][cols, where] = split(y_ref[cols, :])


def end_step(meta, i, m_ref, lhs, rhs, pan, out):
    flat = out.reshape(F * T * 16, T)
    where = pl.ds(pl.multiple_of(i * F * T, F * T), F * T)
    left = lhs[0][where, :], lhs[1][where, :]
    for n in range(0, 2048, 512):
        cols = slice(n, n + 512)
        p = dot3(left, (rhs[0][:, cols], rhs[1][:, cols]))
        for a in range(F):
            for at in range(n // T, n // T + 4):
                lc = (at % 8) * 2 + at // 8
                flat[pl.ds(a * T * 16 + lc, T, stride=16), :] = (
                    m_ref[a, at] - p[a * T : (a + 1) * T, (at * T) % 512 : (at * T) % 512 + T]
                )
    for a in range(F):
        kept = (i * F + a == 0) & (meta[ROW_AT] < 4) & (meta[COL_AT] >= 4)

        @pl.when(jnp.logical_not(kept))
        def _():
            flat[pl.ds(a * T * 16, T, stride=16), :] = pan[i * F + a]


def finish_kernel(meta, ihi, ilo, x0, x1, x2, x3, xc, m_ref, out, lhi, llo, chi, clo, pan, xhi, xlo, yr, yc):
    i = pl.program_id(0)

    @pl.when(i < ROW_STEPS)
    def _():
        rows_step(meta, i, (ihi, ilo), (x0, x1, x2, x3), (lhi, llo), pan, (xhi, xlo), yr)

    @pl.when((i >= ROW_STEPS) & (i < ROW_STEPS + COL_STEPS))
    def _():
        cols_step(i - ROW_STEPS, (ihi, ilo), xc, (chi, clo), yc)

    @pl.when(i >= ROW_STEPS + COL_STEPS)
    def _():
        end_step(meta, i - ROW_STEPS - COL_STEPS, m_ref, (lhi, llo), (chi, clo), pan, out)


def finish(meta, inverse, rows_x, cols_x, m):
    def part(i, before, count):
        return jnp.clip(i - before, 0, count - 1)

    def col_block(i, m):
        j = part(i, ROW_STEPS, COL_STEPS)
        return j // 4, 0, j % 4, 0, 0

    def end_block(i, m):
        return part(i, ROW_STEPS + COL_STEPS, END_STEPS), 0, 0, 0

    whole = pl.BlockSpec((W, W), lambda i, m: (0, 0), pipeline_mode=pl.Buffered(1))
    tiles = pl.BlockSpec((2, H, T, T), lambda i, m: (0, part(i, 0, ROW_STEPS), 0, 0))
    return pl.pallas_call(
        finish_kernel,
        grid_spec=pltpu.PrefetchScalarGridSpec(
            num_scalar_prefetch=1,
            grid=(ROW_STEPS + COL_STEPS + END_STEPS,),
            in_specs=[whole, whole]
            + [tiles] * 4
            + [pl.BlockSpec((None, 8, 2, T, T), col_block), pl.BlockSpec((F, 16, T, T), end_block)],
            out_specs=pl.BlockSpec((F, T, 16, T), end_block),
            scratch_shapes=[
                pltpu.VMEM((W, W), BF16),
                pltpu.VMEM((W, W), BF16),
                pltpu.VMEM((W, 2048), BF16),
                pltpu.VMEM((W, 2048), BF16),
                pltpu.VMEM((8, T, T), F32),
                pltpu.VMEM((H * T, W), BF16),
                pltpu.VMEM((H * T, W), BF16),
                pltpu.VMEM((H * T, W), F32),
                pltpu.VMEM((W, B), F32),
            ],
        ),
        out_shape=jax.ShapeDtypeStruct((8, T, 16, T), F32),
        compiler_params=params(),
        name="finish",
    )(meta, *inverse, *rows_x, cols_x, m)


def exchange(x, axis):
    return lax.all_to_all(x, axis, split_axis=0, concat_axis=0, tiled=True)


def row_id(y, z, core):
    return (y % 2) * 8 + (z % 4) * 2 + core % 2


def col_id(x, y):
    return (x % 4) * 2 + y % 2


def along_row(v, dy, dz, dcore):
    pairs = [
        (row_id(y, z, core), row_id(y + dy, z + dz, core + dcore))
        for y in range(2)
        for z in range(4)
        for core in range(2)
    ]
    return lax.ppermute(v, "row", pairs)


def along_col(v, dx, dy):
    return lax.ppermute(
        v, "col", [(col_id(x, y), col_id(x + dx, y + dy)) for x in range(4) for y in range(2)]
    )


def down(v):
    return lax.ppermute(v, "row", [(i, i + 8) for i in range(8)])


def shards(front, child_blocks, child_map):
    row = lax.axis_index("row")
    col = lax.axis_index("col")
    meta = jnp.concatenate([child_map.reshape(-1), jnp.stack([row, col])]).astype(jnp.int32)
    upper = row < 8

    arrived = exchange(pack_rows(meta, child_blocks), "row")
    landed = exchange(pack_cols(meta, arrived), "col")
    first = assemble(meta, front, landed, 0, 1)[0]

    tile = jnp.where(upper, first[0], down(first[0]))
    two = jnp.stack([tile, along_col(tile, 0, 1)])
    two, first, landed, front = lax.optimization_barrier((two, first, landed, front))
    line = jnp.stack([two] + [along_col(two, dx, 0) for dx in (1, 2, 3)])
    ours = jnp.where(upper, first[:8], down(first[8:]))
    mine = first_col(meta, front, landed)
    line, mine, landed, front = lax.optimization_barrier((line, mine, landed, front))
    parts = [line] + [along_row(line, 0, dz, 0) for dz in (1, 2, 3)]
    pair = jnp.stack([mine, along_col(mine, 0, 1)])
    matrix = assemble(meta, front, landed, 0, 8)
    parts, pair, ours, matrix = lax.optimization_barrier((parts, pair, ours, matrix))
    own = jnp.stack(parts)
    other = along_row(own, 0, 0, 1)

    cols_x = lax.all_gather(ours, "row").reshape(2, 8, 8, T, T)
    other, pair = lax.optimization_barrier((other, pair))
    rows_x = [pair] + [along_col(pair, dx, 0) for dx in (1, 2, 3)]

    inverse = invert(meta, own, other)
    return finish(meta, inverse, rows_x, cols_x, matrix)


def solution(mesh):
    in_specs = (P(None, "row", None, "col"), P(None, None, "row", None, "col"), P())
    out_specs = P(None, "row", None, "col")
    return jax.shard_map(shards, mesh=mesh, in_specs=in_specs, out_specs=out_specs, check_vma=False)
```

```python
import functools

import jax
import jax.numpy as jnp
from jax import lax
from jax.experimental import pallas as pl
from jax.experimental.pallas import tpu as pltpu
from jax.sharding import PartitionSpec as P

T = 128
W = 1024
F32 = jnp.float32
BF16 = jnp.bfloat16
HIGHEST = lax.Precision.HIGHEST
ROW_AT = 128
COL_AT = 129
VMEM = 58 * 1024 * 1024


def params(**kw):
    return pltpu.CompilerParams(vmem_limit_bytes=VMEM, **kw)


def shift(meta, h, k):
    return meta[h * 64 + 16 * k] & 15


def source_row(meta, h, ka):
    return (meta[ROW_AT] - shift(meta, h, ka)) & 15


def local_row(meta, h, ka):
    return meta[h * 64 + source_row(meta, h, ka) + 16 * ka] >> 4


def level_of(meta, h, a):
    ka = jnp.int32(0)
    found = jnp.int32(0)
    for k in range(4):
        hit = local_row(meta, h, k) == a
        ka = jnp.where(hit, k, ka)
        found = jnp.where(hit, 1, found)
    return ka, found


def dest_col(meta, h, kb):
    return (meta[COL_AT] + shift(meta, h, kb)) & 7


def source_col(meta, h, kb):
    return (meta[COL_AT] - shift(meta, h, kb)) & 7


def local_col(meta, h, kb, i):
    return meta[h * 64 + source_col(meta, h, kb) + 8 * (2 * kb + i)] >> 3


def split(x):
    hi = x.astype(BF16)
    return hi, (x - hi.astype(F32)).astype(BF16)


def dot(a, b, dims=((1,), (0,)), precision=None):
    return lax.dot_general(a, b, (dims, ((), ())), precision=precision, preferred_element_type=F32)


NT = ((1,), (1,))


def dot3(a, b, dims=((1,), (0,))):
    return dot(a[0], b[0], dims) + (dot(a[0], b[1], dims) + dot(a[1], b[0], dims))


def pack_rows_kernel(meta, child, out, held, packed, in_sems, out_sems):
    blocks = [(h, k) for h in range(2) for k in range(4)]
    loads = [
        pltpu.make_async_copy(child.at[h, k], held.at[n], in_sems.at[n]) for n, (h, k) in enumerate(blocks)
    ]
    stores = [
        pltpu.make_async_copy(
            packed.at[n], out.at[(meta[ROW_AT] + shift(meta, h, k)) & 15], out_sems.at[n]
        )
        for n, (h, k) in enumerate(blocks)
    ]
    for load in loads:
        load.start()
    flat = held.reshape(8 * T * 8, T)
    for n in range(8):
        loads[n].wait()
        for j in range(8):
            packed[n, j] = flat[pl.ds(n * T * 8 + j, T, stride=8), :]
        stores[n].start()
    for store in stores:
        store.wait()


def pack_rows(meta, child):
    return pl.pallas_call(
        pack_rows_kernel,
        in_specs=[pl.BlockSpec(memory_space=pltpu.SMEM), pl.BlockSpec(memory_space=pl.ANY)],
        out_specs=pl.BlockSpec(memory_space=pl.ANY),
        out_shape=jax.ShapeDtypeStruct((16, 8, T, T), F32),
        scratch_shapes=[
            pltpu.VMEM((8, T, 8, T), F32),
            pltpu.VMEM((8, 8, T, T), F32),
            pltpu.SemaphoreType.DMA((8,)),
            pltpu.SemaphoreType.DMA((8,)),
        ],
        compiler_params=params(),
        name="pack_rows",
    )(meta, child)


def pack_cols_kernel(meta, arrived, out, held, in_sems, out_sems):
    pairs = [(h, kb) for h in range(2) for kb in range(4)]
    loads = [
        [
            pltpu.make_async_copy(
                arrived.at[source_row(meta, h, lev), pl.ds(2 * kb, 2)],
                held.at[n, lev],
                in_sems.at[n, lev],
            )
            for lev in range(4)
        ]
        for n, (h, kb) in enumerate(pairs)
    ]
    stores = [
        pltpu.make_async_copy(held.at[n], out.at[dest_col(meta, h, kb), h], out_sems.at[n])
        for n, (h, kb) in enumerate(pairs)
    ]
    for group in loads:
        for load in group:
            load.start()
    for n in range(8):
        for load in loads[n]:
            load.wait()
        stores[n].start()
    for store in stores:
        store.wait()


def pack_cols(meta, arrived):
    return pl.pallas_call(
        pack_cols_kernel,
        in_specs=[pl.BlockSpec(memory_space=pltpu.SMEM), pl.BlockSpec(memory_space=pl.ANY)],
        out_specs=pl.BlockSpec(memory_space=pl.ANY),
        out_shape=jax.ShapeDtypeStruct((8, 2, 4, 2, T, T), F32),
        scratch_shapes=[
            pltpu.VMEM((8, 4, 2, T, T), F32),
            pltpu.SemaphoreType.DMA((8, 4)),
            pltpu.SemaphoreType.DMA((8,)),
        ],
        compiler_params=params(),
        name="pack_cols",
    )(meta, arrived)


def place(lc):
    return (lc & 1) * 8 + (lc >> 1)


def assemble_kernel(start, meta, front_ref, *refs):
    tiles, out_ref = refs[:-1], refs[-1]
    flat = front_ref.reshape(T * 16, T)
    for lc in range(16):
        out_ref[place(lc)] = flat[pl.ds(lc, T, stride=16), :]
    for h in range(2):
        _, found = level_of(meta, h, start + pl.program_id(0))

        @pl.when(found == 1)
        def _():
            for kb in range(4):
                for i in range(2):
                    at = place(local_col(meta, h, kb, i))
                    out_ref[at] = out_ref[at] + tiles[4 * h + kb][i]


def assemble(meta, front, landed, start, count):
    def tile_spec(h, kb):
        return pl.BlockSpec(
            (None, None, None, 2, T, T),
            lambda i, m: (source_col(m, h, kb), h, level_of(m, h, start + i)[0], 0, 0, 0),
        )

    return pl.pallas_call(
        functools.partial(assemble_kernel, start),
        grid_spec=pltpu.PrefetchScalarGridSpec(
            num_scalar_prefetch=1,
            grid=(count,),
            in_specs=[pl.BlockSpec((None, T, 16, T), lambda i, m: (start + i, 0, 0, 0))]
            + [tile_spec(h, kb) for h in range(2) for kb in range(4)],
            out_specs=pl.BlockSpec((None, 16, T, T), lambda i, m: (i, 0, 0, 0)),
        ),
        out_shape=jax.ShapeDtypeStruct((count, 16, T, T), F32),
        compiler_params=params(),
        cost_estimate=pl.CostEstimate(flops=0, bytes_accessed=count * 5 << 19, transcendentals=0),
        name=f"assemble_{count}",
    )(meta, front, *([landed] * 8))


def tile_of_first_col(meta, h):
    at = jnp.int32(0)
    found = jnp.int32(0)
    for kb in range(4):
        for i in range(2):
            hit = local_col(meta, h, kb, i) == 0
            at = jnp.where(hit, 2 * kb + i, at)
            found = jnp.where(hit, 1, found)
    return at >> 1, at & 1, found


def first_col_kernel(meta, front_ref, *refs):
    tiles, out_ref = refs[:-1], refs[-1]
    flat = front_ref.reshape(8 * T * 8, T)
    for a in range(8):
        out_ref[a] = flat[pl.ds(a * T * 8, T, stride=8), :]
    for h in range(2):
        _, _, found = tile_of_first_col(meta, h)

        @pl.when(found == 1)
        def _():
            for ka in range(4):
                a = local_row(meta, h, ka)
                out_ref[a] = out_ref[a] + tiles[4 * h + ka][...]


def first_col(meta, front, landed):
    def tile_spec(h, ka):
        def at(i, m):
            kb, j, _ = tile_of_first_col(m, h)
            return source_col(m, h, kb), h, ka, j, 0, 0

        return pl.BlockSpec((None, None, None, None, T, T), at)

    whole = pl.BlockSpec((8, T, T), lambda i, m: (0, 0, 0))
    return pl.pallas_call(
        first_col_kernel,
        grid_spec=pltpu.PrefetchScalarGridSpec(
            num_scalar_prefetch=1,
            grid=(1,),
            in_specs=[pl.BlockSpec((8, T, 8, T), lambda i, m: (0, 0, 0, 0))]
            + [tile_spec(h, ka) for h in range(2) for ka in range(4)],
            out_specs=whole,
        ),
        out_shape=jax.ShapeDtypeStruct((8, T, T), F32),
        compiler_params=params(),
        name="first_col",
    )(meta, front, *([landed] * 8))


def root(x):
    r = lax.rsqrt(x)
    return r * (1.5 - 0.5 * x * r * r)


def inverse_of(x):
    return pl.reciprocal(x, approx=False)


def invert_kernel(meta, own, other, hi_ref, lo_ref, a_ref, t_ref, l_ref):
    row, col = meta[ROW_AT], meta[COL_AT]
    for q in range(8):
        same = ((row ^ q) & 1) == 0
        dz = ((row >> 1) - (q >> 1)) & 3
        for c in range(8):
            at = (dz, ((col >> 1) - (c >> 1)) & 3, (col ^ c) & 1)
            a_ref[q * T : (q + 1) * T, c * T : (c + 1) * T] = jnp.where(same, own[at], other[at])
    t_ref[...] = jnp.zeros_like(t_ref)
    sub = lax.broadcasted_iota(jnp.int32, (8, T), 0)
    lane = lax.broadcasted_iota(jnp.int32, (8, T), 1)

    def over(x):
        return jnp.broadcast_to(x, (8, T))

    def step(k, _):
        at = pl.multiple_of(k * T, T)
        s = [a_ref[pl.ds(at + 8 * b, 8), pl.ds(at, T)] for b in range(16)]
        on_diagonal = [lane == sub + 8 * b for b in range(16)]
        only = [jnp.where(on_diagonal[b], s[b], F32(0)) for b in range(16)]
        total = only[0]
        for b in range(1, 16):
            total = total + only[b]
        by_lane = over(root(jnp.sum(total, axis=0, keepdims=True)))
        s = [s[b] * (over(root(jnp.sum(only[b], axis=1, keepdims=True))) * by_lane) for b in range(16)]
        t = [jnp.where(on_diagonal[b], F32(1), F32(0)) for b in range(16)]
        for j in range(0, T, 4):
            b0, i0 = divmod(j, 8)
            p = [[over(s[b0][i0 + i : i0 + i + 1, j + c : j + c + 1]) for c in range(i + 1)] for i in range(4)]
            sr = [over(s[b0][i0 + i : i0 + i + 1, :]) for i in range(4)]
            tr = [over(t[b0][i0 + i : i0 + i + 1, :]) for i in range(4)]
            (p00,), (p10, p11), (p20, p21, p22), (p30, p31, p32, p33) = p
            first = inverse_of(p00 * p11 - p10 * p10)
            x20 = (p20 * p11 - p21 * p10) * first
            x21 = (p21 * p00 - p20 * p10) * first
            x30 = (p30 * p11 - p31 * p10) * first
            x31 = (p31 * p00 - p30 * p10) * first
            s22 = p22 - (x20 * p20 + x21 * p21)
            s32 = p32 - (x30 * p20 + x31 * p21)
            s33 = p33 - (x30 * p30 + x31 * p31)
            second = inverse_of(s22 * s33 - s32 * s32)
            y00, y10, y11 = p11 * first, p10 * first, p00 * first
            y22, y32, y33 = s33 * second, s32 * second, s22 * second

            def solved(rows):
                r2 = rows[2] - (x20 * rows[0] + x21 * rows[1])
                r3 = rows[3] - (x30 * rows[0] + x31 * rows[1])
                z2 = y22 * r2 - y32 * r3
                z3 = y33 * r3 - y32 * r2
                z0 = (y00 * rows[0] - y10 * rows[1]) - (x20 * z2 + x30 * z3)
                z1 = (y11 * rows[1] - y10 * rows[0]) - (x21 * z2 + x31 * z3)
                return (z0, z1, z2, z3), r2, r3

            zs, _, _ = solved(sr)
            zt, t2, t3 = solved(tr)
            r0 = root(p00)
            l10 = p10 * r0
            r1 = root(p11 - l10 * l10)
            r2 = root(s22)
            l32 = s32 * r2
            r3 = root(s33 - l32 * l32)
            done = (
                tr[0] * r0,
                (tr[1] - l10 * r0 * tr[0]) * r1,
                t2 * r2,
                (t3 - l32 * r2 * t2) * r3,
            )
            for b in range(b0 if i0 == 0 else b0 + 1, 16):
                v = [over(s[b][:, j + c : j + c + 1]) for c in range(4)]
                if b == b0:
                    v = [jnp.where(sub > 3, x, F32(0)) for x in v]
                s[b] = s[b] - ((v[0] * zs[0] + v[1] * zs[1]) + (v[2] * zs[2] + v[3] * zs[3]))
                t[b] = t[b] - ((v[0] * zt[0] + v[1] * zt[1]) + (v[2] * zt[2] + v[3] * zt[3]))
            for i in range(4):
                t[b0] = jnp.where(sub == i0 + i, done[i], t[b0])
        t = [x * by_lane for x in t]
        kinv = jnp.concatenate(t, axis=0)
        for kk in range(8):

            @pl.when(k == kk)
            def _():
                lo, hi = kk * T, (kk + 1) * T
                if kk:
                    t_ref[lo:hi, :lo] = dot(kinv, t_ref[lo:hi, :lo], precision=HIGHEST)
                t_ref[lo:hi, lo:hi] = kinv
                if kk < 7:
                    col = dot(a_ref[hi:, lo:hi], kinv, NT, precision=HIGHEST)
                    l_ref[hi:, :] = col
                    for n0 in range(hi, W, T):
                        a_ref[n0:, n0 : n0 + T] = a_ref[n0:, n0 : n0 + T] - dot(
                            l_ref[n0:, :], l_ref[n0 : n0 + T, :], NT, precision=HIGHEST
                        )
                    t_ref[hi:, :hi] = t_ref[hi:, :hi] - dot(
                        l_ref[hi:, :], t_ref[lo:hi, :hi], precision=HIGHEST
                    )

        return 0

    lax.fori_loop(0, 8, step, 0)
    hi_ref[...], lo_ref[...] = split(t_ref[...])


def invert(meta, own, other):
    whole = pl.BlockSpec(memory_space=pltpu.VMEM)
    return pl.pallas_call(
        invert_kernel,
        in_specs=[pl.BlockSpec(memory_space=pltpu.SMEM), whole, whole],
        out_specs=[whole, whole],
        out_shape=[jax.ShapeDtypeStruct((W, W), BF16)] * 2,
        scratch_shapes=[
            pltpu.VMEM((W, W), F32),
            pltpu.VMEM((W, W), F32),
            pltpu.VMEM((W, T), F32),
        ],
        compiler_params=params(),
        cost_estimate=pl.CostEstimate(flops=80_000_000_000, bytes_accessed=8 << 20, transcendentals=0),
        name="invert",
    )(meta, own, other)


B = 512
K = 256
H = 4
F = 2
ROW_STEPS = 8 // H
COL_STEPS = 2048 // B
END_STEPS = 8 // F


def rows_step(meta, i, inverse, xs, lhs, pan, x_refs, y_ref):
    ihi, ilo = inverse
    xhi, xlo = x_refs
    for d in range(8):
        q = (((meta[COL_AT] >> 1) - (d >> 1)) & 3) * 2 + ((meta[COL_AT] ^ d) & 1)
        cols = pl.ds(pl.multiple_of(q * T, T), T)
        for a in range(H):
            rows = slice(a * T, (a + 1) * T)
            xhi[rows, cols], xlo[rows, cols] = split(xs[d >> 1][d & 1, a])
    for k in range(W // K):
        n = (k + 1) * K
        rows = slice(k * K, n)
        y_ref[:, rows] = dot3((xhi[:, :n], xlo[:, :n]), (ihi[rows, :n], ilo[rows, :n]), NT)
    at = pl.multiple_of(meta[COL_AT] * T, T)
    for a in range(H):
        pan[i * H + a] = y_ref[a * T : (a + 1) * T, pl.ds(at, T)]
    row = meta[ROW_AT]
    limit = jnp.where(row < 4, 0, jnp.where(row < 8, 512, W))
    limit = jnp.where(i == 0, limit, W)
    inside = lax.broadcasted_iota(jnp.int32, (T, W), 1) < limit
    y_ref[:T, :] = jnp.where(inside, y_ref[:T, :], F32(0))
    where = pl.ds(pl.multiple_of(i * H * T, H * T), H * T)
    lhs[0][where, :], lhs[1][where, :] = split(y_ref[...])


def cols_step(i, inverse, x_ref, rhs, y_ref):
    ihi, ilo = inverse
    where = pl.ds(pl.multiple_of(i * B, B), B)
    for k in range(W // K):
        x = jnp.concatenate(
            [
                jnp.concatenate([x_ref[q, n] for n in range(B // T)], axis=1)
                for q in range(k * K // T, (k + 1) * K // T)
            ],
            axis=0,
        )
        cols = slice(k * K, (k + 1) * K)
        y = dot3((ihi[k * K :, cols], ilo[k * K :, cols]), split(x))
        y_ref[k * K :, :] = y if k == 0 else y_ref[k * K :, :] + y
        rhs[0][cols, where], rhs[1][cols, where] = split(y_ref[cols, :])


def end_step(meta, i, m_ref, lhs, rhs, pan, out):
    flat = out.reshape(F * T * 16, T)
    where = pl.ds(pl.multiple_of(i * F * T, F * T), F * T)
    left = lhs[0][where, :], lhs[1][where, :]
    for n in range(0, 2048, 512):
        cols = slice(n, n + 512)
        p = dot3(left, (rhs[0][:, cols], rhs[1][:, cols]))
        for a in range(F):
            for at in range(n // T, n // T + 4):
                lc = (at % 8) * 2 + at // 8
                flat[pl.ds(a * T * 16 + lc, T, stride=16), :] = (
                    m_ref[a, at] - p[a * T : (a + 1) * T, (at * T) % 512 : (at * T) % 512 + T]
                )
    for a in range(F):
        kept = (i * F + a == 0) & (meta[ROW_AT] < 4) & (meta[COL_AT] >= 4)

        @pl.when(jnp.logical_not(kept))
        def _():
            flat[pl.ds(a * T * 16, T, stride=16), :] = pan[i * F + a]


def finish_kernel(meta, ihi, ilo, x0, x1, x2, x3, xc, m_ref, out, lhi, llo, chi, clo, pan, xhi, xlo, yr, yc):
    i = pl.program_id(0)

    @pl.when(i < ROW_STEPS)
    def _():
        rows_step(meta, i, (ihi, ilo), (x0, x1, x2, x3), (lhi, llo), pan, (xhi, xlo), yr)

    @pl.when((i >= ROW_STEPS) & (i < ROW_STEPS + COL_STEPS))
    def _():
        cols_step(i - ROW_STEPS, (ihi, ilo), xc, (chi, clo), yc)

    @pl.when(i >= ROW_STEPS + COL_STEPS)
    def _():
        end_step(meta, i - ROW_STEPS - COL_STEPS, m_ref, (lhi, llo), (chi, clo), pan, out)


def finish(meta, inverse, rows_x, cols_x, m):
    def part(i, before, count):
        return jnp.clip(i - before, 0, count - 1)

    def col_block(i, m):
        j = part(i, ROW_STEPS, COL_STEPS)
        return j // (1024 // B), 0, j % (1024 // B), 0, 0

    def end_block(i, m):
        return part(i, ROW_STEPS + COL_STEPS, END_STEPS), 0, 0, 0

    whole = pl.BlockSpec((W, W), lambda i, m: (0, 0), pipeline_mode=pl.Buffered(1))
    tiles = pl.BlockSpec((2, H, T, T), lambda i, m: (0, part(i, 0, ROW_STEPS), 0, 0))
    return pl.pallas_call(
        finish_kernel,
        grid_spec=pltpu.PrefetchScalarGridSpec(
            num_scalar_prefetch=1,
            grid=(ROW_STEPS + COL_STEPS + END_STEPS,),
            in_specs=[whole, whole]
            + [tiles] * 4
            + [pl.BlockSpec((None, 8, B // T, T, T), col_block), pl.BlockSpec((F, 16, T, T), end_block)],
            out_specs=pl.BlockSpec((F, T, 16, T), end_block),
            scratch_shapes=[
                pltpu.VMEM((W, W), BF16),
                pltpu.VMEM((W, W), BF16),
                pltpu.VMEM((W, 2048), BF16),
                pltpu.VMEM((W, 2048), BF16),
                pltpu.VMEM((8, T, T), F32),
                pltpu.VMEM((H * T, W), BF16),
                pltpu.VMEM((H * T, W), BF16),
                pltpu.VMEM((H * T, W), F32),
                pltpu.VMEM((W, B), F32),
            ],
        ),
        out_shape=jax.ShapeDtypeStruct((8, T, 16, T), F32),
        compiler_params=params(),
        name="finish",
    )(meta, *inverse, *rows_x, cols_x, m)


def exchange(x, axis):
    return lax.all_to_all(x, axis, split_axis=0, concat_axis=0, tiled=True)


def row_id(y, z, core):
    return (y % 2) * 8 + (z % 4) * 2 + core % 2


def col_id(x, y):
    return (x % 4) * 2 + y % 2


def along_row(v, dy, dz, dcore):
    pairs = [
        (row_id(y, z, core), row_id(y + dy, z + dz, core + dcore))
        for y in range(2)
        for z in range(4)
        for core in range(2)
    ]
    return lax.ppermute(v, "row", pairs)


def along_col(v, dx, dy):
    return lax.ppermute(
        v, "col", [(col_id(x, y), col_id(x + dx, y + dy)) for x in range(4) for y in range(2)]
    )


def down(v):
    return lax.ppermute(v, "row", [(i, i + 8) for i in range(8)])


def shards(front, child_blocks, child_map):
    row = lax.axis_index("row")
    col = lax.axis_index("col")
    meta = jnp.concatenate([child_map.reshape(-1), jnp.stack([row, col])]).astype(jnp.int32)
    upper = row < 8

    arrived = exchange(pack_rows(meta, child_blocks), "row")
    landed = exchange(pack_cols(meta, arrived), "col")
    first = assemble(meta, front, landed, 0, 1)[0]

    tile = jnp.where(upper, first[0], down(first[0]))
    two = jnp.stack([tile, along_col(tile, 0, 1)])
    two, first, landed, front = lax.optimization_barrier((two, first, landed, front))
    line = jnp.stack([two] + [along_col(two, dx, 0) for dx in (1, 2, 3)])
    ours = jnp.where(upper, first[:8], down(first[8:]))
    mine = first_col(meta, front, landed)
    line, mine, landed, front = lax.optimization_barrier((line, mine, landed, front))
    parts = [line] + [along_row(line, 0, dz, 0) for dz in (1, 2, 3)]
    pair = jnp.stack([mine, along_col(mine, 0, 1)])
    matrix = assemble(meta, front, landed, 0, 8)
    parts, pair, ours, matrix = lax.optimization_barrier((parts, pair, ours, matrix))
    own = jnp.stack(parts)
    other = along_row(own, 0, 0, 1)

    cols_x = lax.all_gather(ours, "row").reshape(2, 8, 8, T, T)
    other, pair = lax.optimization_barrier((other, pair))
    rows_x = [pair] + [along_col(pair, dx, 0) for dx in (1, 2, 3)]

    inverse = invert(meta, own, other)
    return finish(meta, inverse, rows_x, cols_x, matrix)


def solution(mesh):
    in_specs = (P(None, "row", None, "col"), P(None, None, "row", None, "col"), P())
    out_specs = P(None, "row", None, "col")
    return jax.shard_map(shards, mesh=mesh, in_specs=in_specs, out_specs=out_specs, check_vma=False)
```

```python
import functools

import jax
import jax.numpy as jnp
from jax import lax
from jax.experimental import pallas as pl
from jax.experimental.pallas import tpu as pltpu
from jax.sharding import PartitionSpec as P

T = 128
W = 1024
F32 = jnp.float32
BF16 = jnp.bfloat16
HIGHEST = lax.Precision.HIGHEST
ROW_AT = 128
COL_AT = 129
VMEM = 58 * 1024 * 1024


def params(**kw):
    return pltpu.CompilerParams(vmem_limit_bytes=VMEM, **kw)


def shift(meta, h, k):
    return meta[h * 64 + 16 * k] & 15


def source_row(meta, h, ka):
    return (meta[ROW_AT] - shift(meta, h, ka)) & 15


def local_row(meta, h, ka):
    return meta[h * 64 + source_row(meta, h, ka) + 16 * ka] >> 4


def level_of(meta, h, a):
    ka = jnp.int32(0)
    found = jnp.int32(0)
    for k in range(4):
        hit = local_row(meta, h, k) == a
        ka = jnp.where(hit, k, ka)
        found = jnp.where(hit, 1, found)
    return ka, found


def dest_col(meta, h, kb):
    return (meta[COL_AT] + shift(meta, h, kb)) & 7


def source_col(meta, h, kb):
    return (meta[COL_AT] - shift(meta, h, kb)) & 7


def local_col(meta, h, kb, i):
    return meta[h * 64 + source_col(meta, h, kb) + 8 * (2 * kb + i)] >> 3


def split(x):
    hi = x.astype(BF16)
    return hi, (x - hi.astype(F32)).astype(BF16)


def dot(a, b, dims=((1,), (0,)), precision=None):
    return lax.dot_general(a, b, (dims, ((), ())), precision=precision, preferred_element_type=F32)


NT = ((1,), (1,))


def dot3(a, b, dims=((1,), (0,))):
    return dot(a[0], b[0], dims) + (dot(a[0], b[1], dims) + dot(a[1], b[0], dims))


def pack_rows_kernel(meta, child, out, held, packed, in_sems, out_sems):
    blocks = [(h, k) for h in range(2) for k in range(4)]
    loads = [
        pltpu.make_async_copy(child.at[h, k], held.at[n], in_sems.at[n]) for n, (h, k) in enumerate(blocks)
    ]
    stores = [
        pltpu.make_async_copy(
            packed.at[n], out.at[(meta[ROW_AT] + shift(meta, h, k)) & 15], out_sems.at[n]
        )
        for n, (h, k) in enumerate(blocks)
    ]
    for load in loads:
        load.start()
    flat = held.reshape(8 * T * 8, T)
    for n in range(8):
        loads[n].wait()
        for j in range(8):
            packed[n, j] = flat[pl.ds(n * T * 8 + j, T, stride=8), :]
        stores[n].start()
    for store in stores:
        store.wait()


def pack_rows(meta, child):
    return pl.pallas_call(
        pack_rows_kernel,
        in_specs=[pl.BlockSpec(memory_space=pltpu.SMEM), pl.BlockSpec(memory_space=pl.ANY)],
        out_specs=pl.BlockSpec(memory_space=pl.ANY),
        out_shape=jax.ShapeDtypeStruct((16, 8, T, T), F32),
        scratch_shapes=[
            pltpu.VMEM((8, T, 8, T), F32),
            pltpu.VMEM((8, 8, T, T), F32),
            pltpu.SemaphoreType.DMA((8,)),
            pltpu.SemaphoreType.DMA((8,)),
        ],
        compiler_params=params(),
        name="pack_rows",
    )(meta, child)


def pack_cols_kernel(meta, arrived, out, held, in_sems, out_sems):
    pairs = [(h, kb) for h in range(2) for kb in range(4)]
    loads = [
        [
            pltpu.make_async_copy(
                arrived.at[source_row(meta, h, lev), pl.ds(2 * kb, 2)],
                held.at[n, lev],
                in_sems.at[n, lev],
            )
            for lev in range(4)
        ]
        for n, (h, kb) in enumerate(pairs)
    ]
    stores = [
        pltpu.make_async_copy(held.at[n], out.at[dest_col(meta, h, kb), h], out_sems.at[n])
        for n, (h, kb) in enumerate(pairs)
    ]
    for group in loads:
        for load in group:
            load.start()
    for n in range(8):
        for load in loads[n]:
            load.wait()
        stores[n].start()
    for store in stores:
        store.wait()


def pack_cols(meta, arrived):
    return pl.pallas_call(
        pack_cols_kernel,
        in_specs=[pl.BlockSpec(memory_space=pltpu.SMEM), pl.BlockSpec(memory_space=pl.ANY)],
        out_specs=pl.BlockSpec(memory_space=pl.ANY),
        out_shape=jax.ShapeDtypeStruct((8, 2, 4, 2, T, T), F32),
        scratch_shapes=[
            pltpu.VMEM((8, 4, 2, T, T), F32),
            pltpu.SemaphoreType.DMA((8, 4)),
            pltpu.SemaphoreType.DMA((8,)),
        ],
        compiler_params=params(),
        name="pack_cols",
    )(meta, arrived)


def place(lc):
    return (lc & 1) * 8 + (lc >> 1)


def assemble_kernel(start, meta, front_ref, *refs):
    tiles, out_ref = refs[:-1], refs[-1]
    flat = front_ref.reshape(T * 16, T)
    for lc in range(16):
        out_ref[place(lc)] = flat[pl.ds(lc, T, stride=16), :]
    for h in range(2):
        _, found = level_of(meta, h, start + pl.program_id(0))

        @pl.when(found == 1)
        def _():
            for kb in range(4):
                for i in range(2):
                    at = place(local_col(meta, h, kb, i))
                    out_ref[at] = out_ref[at] + tiles[4 * h + kb][i]


def assemble(meta, front, landed, start, count):
    def tile_spec(h, kb):
        return pl.BlockSpec(
            (None, None, None, 2, T, T),
            lambda i, m: (source_col(m, h, kb), h, level_of(m, h, start + i)[0], 0, 0, 0),
        )

    return pl.pallas_call(
        functools.partial(assemble_kernel, start),
        grid_spec=pltpu.PrefetchScalarGridSpec(
            num_scalar_prefetch=1,
            grid=(count,),
            in_specs=[pl.BlockSpec((None, T, 16, T), lambda i, m: (start + i, 0, 0, 0))]
            + [tile_spec(h, kb) for h in range(2) for kb in range(4)],
            out_specs=pl.BlockSpec((None, 16, T, T), lambda i, m: (i, 0, 0, 0)),
        ),
        out_shape=jax.ShapeDtypeStruct((count, 16, T, T), F32),
        compiler_params=params(),
        cost_estimate=pl.CostEstimate(flops=0, bytes_accessed=count * 5 << 19, transcendentals=0),
        name=f"assemble_{count}",
    )(meta, front, *([landed] * 8))


def tile_of_first_col(meta, h):
    at = jnp.int32(0)
    found = jnp.int32(0)
    for kb in range(4):
        for i in range(2):
            hit = local_col(meta, h, kb, i) == 0
            at = jnp.where(hit, 2 * kb + i, at)
            found = jnp.where(hit, 1, found)
    return at >> 1, at & 1, found


def first_col_kernel(meta, front_ref, *refs):
    tiles, out_ref = refs[:-1], refs[-1]
    flat = front_ref.reshape(8 * T * 8, T)
    for a in range(8):
        out_ref[a] = flat[pl.ds(a * T * 8, T, stride=8), :]
    for h in range(2):
        _, _, found = tile_of_first_col(meta, h)

        @pl.when(found == 1)
        def _():
            for ka in range(4):
                a = local_row(meta, h, ka)
                out_ref[a] = out_ref[a] + tiles[4 * h + ka][...]


def first_col(meta, front, landed):
    def tile_spec(h, ka):
        def at(i, m):
            kb, j, _ = tile_of_first_col(m, h)
            return source_col(m, h, kb), h, ka, j, 0, 0

        return pl.BlockSpec((None, None, None, None, T, T), at)

    whole = pl.BlockSpec((8, T, T), lambda i, m: (0, 0, 0))
    return pl.pallas_call(
        first_col_kernel,
        grid_spec=pltpu.PrefetchScalarGridSpec(
            num_scalar_prefetch=1,
            grid=(1,),
            in_specs=[pl.BlockSpec((8, T, 8, T), lambda i, m: (0, 0, 0, 0))]
            + [tile_spec(h, ka) for h in range(2) for ka in range(4)],
            out_specs=whole,
        ),
        out_shape=jax.ShapeDtypeStruct((8, T, T), F32),
        compiler_params=params(),
        name="first_col",
    )(meta, front, *([landed] * 8))


def root(x):
    r = lax.rsqrt(x)
    return r * (1.5 - 0.5 * x * r * r)


def inverse_of(x):
    return pl.reciprocal(x, approx=False)


def invert_kernel(meta, own, other, hi_ref, lo_ref, a_ref, t_ref, l_ref):
    row, col = meta[ROW_AT], meta[COL_AT]
    for q in range(8):
        same = ((row ^ q) & 1) == 0
        dz = ((row >> 1) - (q >> 1)) & 3
        for c in range(8):
            at = (dz, ((col >> 1) - (c >> 1)) & 3, (col ^ c) & 1)
            a_ref[q * T : (q + 1) * T, c * T : (c + 1) * T] = jnp.where(same, own[at], other[at])
    t_ref[...] = jnp.zeros_like(t_ref)
    sub = lax.broadcasted_iota(jnp.int32, (8, T), 0)
    lane = lax.broadcasted_iota(jnp.int32, (8, T), 1)

    def over(x):
        return jnp.broadcast_to(x, (8, T))

    def step(k, _):
        at = pl.multiple_of(k * T, T)
        s = [a_ref[pl.ds(at + 8 * b, 8), pl.ds(at, T)] for b in range(16)]
        on_diagonal = [lane == sub + 8 * b for b in range(16)]
        only = [jnp.where(on_diagonal[b], s[b], F32(0)) for b in range(16)]
        total = only[0]
        for b in range(1, 16):
            total = total + only[b]
        by_lane = over(root(jnp.sum(total, axis=0, keepdims=True)))
        s = [s[b] * (over(root(jnp.sum(only[b], axis=1, keepdims=True))) * by_lane) for b in range(16)]
        t = [jnp.where(on_diagonal[b], F32(1), F32(0)) for b in range(16)]
        for j in range(0, T, 4):
            b0, i0 = divmod(j, 8)
            p = [[over(s[b0][i0 + i : i0 + i + 1, j + c : j + c + 1]) for c in range(i + 1)] for i in range(4)]
            sr = [over(s[b0][i0 + i : i0 + i + 1, :]) for i in range(4)]
            tr = [over(t[b0][i0 + i : i0 + i + 1, :]) for i in range(4)]
            (p00,), (p10, p11), (p20, p21, p22), (p30, p31, p32, p33) = p
            first = inverse_of(p00 * p11 - p10 * p10)
            x20 = (p20 * p11 - p21 * p10) * first
            x21 = (p21 * p00 - p20 * p10) * first
            x30 = (p30 * p11 - p31 * p10) * first
            x31 = (p31 * p00 - p30 * p10) * first
            s22 = p22 - (x20 * p20 + x21 * p21)
            s32 = p32 - (x30 * p20 + x31 * p21)
            s33 = p33 - (x30 * p30 + x31 * p31)
            second = inverse_of(s22 * s33 - s32 * s32)
            y00, y10, y11 = p11 * first, p10 * first, p00 * first
            y22, y32, y33 = s33 * second, s32 * second, s22 * second

            def solved(rows):
                r2 = rows[2] - (x20 * rows[0] + x21 * rows[1])
                r3 = rows[3] - (x30 * rows[0] + x31 * rows[1])
                z2 = y22 * r2 - y32 * r3
                z3 = y33 * r3 - y32 * r2
                z0 = (y00 * rows[0] - y10 * rows[1]) - (x20 * z2 + x30 * z3)
                z1 = (y11 * rows[1] - y10 * rows[0]) - (x21 * z2 + x31 * z3)
                return (z0, z1, z2, z3), r2, r3

            zs, _, _ = solved(sr)
            zt, t2, t3 = solved(tr)
            r0 = root(p00)
            l10 = p10 * r0
            r1 = root(p11 - l10 * l10)
            r2 = root(s22)
            l32 = s32 * r2
            r3 = root(s33 - l32 * l32)
            done = (
                tr[0] * r0,
                (tr[1] - l10 * r0 * tr[0]) * r1,
                t2 * r2,
                (t3 - l32 * r2 * t2) * r3,
            )
            for b in range(b0 if i0 == 0 else b0 + 1, 16):
                v = [over(s[b][:, j + c : j + c + 1]) for c in range(4)]
                if b == b0:
                    v = [jnp.where(sub > 3, x, F32(0)) for x in v]
                s[b] = s[b] - ((v[0] * zs[0] + v[1] * zs[1]) + (v[2] * zs[2] + v[3] * zs[3]))
                t[b] = t[b] - ((v[0] * zt[0] + v[1] * zt[1]) + (v[2] * zt[2] + v[3] * zt[3]))
            for i in range(4):
                t[b0] = jnp.where(sub == i0 + i, done[i], t[b0])
        t = [x * by_lane for x in t]
        kinv = jnp.concatenate(t, axis=0)
        for kk in range(8):

            @pl.when(k == kk)
            def _():
                lo, hi = kk * T, (kk + 1) * T
                if kk:
                    t_ref[lo:hi, :lo] = dot(kinv, t_ref[lo:hi, :lo], precision=HIGHEST)
                t_ref[lo:hi, lo:hi] = kinv
                if kk < 7:
                    col = dot(a_ref[hi:, lo:hi], kinv, NT, precision=HIGHEST)
                    l_ref[hi:, :] = col
                    for n0 in range(hi, W, T):
                        a_ref[n0:, n0 : n0 + T] = a_ref[n0:, n0 : n0 + T] - dot(
                            l_ref[n0:, :], l_ref[n0 : n0 + T, :], NT, precision=HIGHEST
                        )
                    t_ref[hi:, :hi] = t_ref[hi:, :hi] - dot(
                        l_ref[hi:, :], t_ref[lo:hi, :hi], precision=HIGHEST
                    )

        return 0

    lax.fori_loop(0, 8, step, 0)
    hi_ref[...], lo_ref[...] = split(t_ref[...])


def invert(meta, own, other):
    whole = pl.BlockSpec(memory_space=pltpu.VMEM)
    return pl.pallas_call(
        invert_kernel,
        in_specs=[pl.BlockSpec(memory_space=pltpu.SMEM), whole, whole],
        out_specs=[whole, whole],
        out_shape=[jax.ShapeDtypeStruct((W, W), BF16)] * 2,
        scratch_shapes=[
            pltpu.VMEM((W, W), F32),
            pltpu.VMEM((W, W), F32),
            pltpu.VMEM((W, T), F32),
        ],
        compiler_params=params(),
        cost_estimate=pl.CostEstimate(flops=80_000_000_000, bytes_accessed=8 << 20, transcendentals=0),
        name="invert",
    )(meta, own, other)


B = 512
K = 256
H = 4
F = 2
ROW_STEPS = 8 // H
COL_STEPS = 2048 // B
END_STEPS = 8 // F


def rows_step(meta, i, inverse, xs, lhs, pan, x_refs, y_ref):
    ihi, ilo = inverse
    xhi, xlo = x_refs
    for d in range(8):
        q = (((meta[COL_AT] >> 1) - (d >> 1)) & 3) * 2 + ((meta[COL_AT] ^ d) & 1)
        cols = pl.ds(pl.multiple_of(q * T, T), T)
        for a in range(H):
            rows = slice(a * T, (a + 1) * T)
            xhi[rows, cols], xlo[rows, cols] = split(xs[d >> 1][d & 1, a])
    for k in range(W // K):
        n = (k + 1) * K
        rows = slice(k * K, n)
        y_ref[:, rows] = dot3((xhi[:, :n], xlo[:, :n]), (ihi[rows, :n], ilo[rows, :n]), NT)
    at = pl.multiple_of(meta[COL_AT] * T, T)
    for a in range(H):
        pan[i * H + a] = y_ref[a * T : (a + 1) * T, pl.ds(at, T)]
    row = meta[ROW_AT]
    limit = jnp.where(row < 4, 0, jnp.where(row < 8, 512, W))
    limit = jnp.where(i == 0, limit, W)
    inside = lax.broadcasted_iota(jnp.int32, (T, W), 1) < limit
    y_ref[:T, :] = jnp.where(inside, y_ref[:T, :], F32(0))
    where = pl.ds(pl.multiple_of(i * H * T, H * T), H * T)
    lhs[0][where, :], lhs[1][where, :] = split(y_ref[...])


def cols_step(i, inverse, x_ref, rhs, y_ref):
    ihi, ilo = inverse
    where = pl.ds(pl.multiple_of(i * B, B), B)
    for k in range(W // K):
        x = jnp.concatenate(
            [
                jnp.concatenate([x_ref[q, n] for n in range(B // T)], axis=1)
                for q in range(k * K // T, (k + 1) * K // T)
            ],
            axis=0,
        )
        cols = slice(k * K, (k + 1) * K)
        y = dot3((ihi[k * K :, cols], ilo[k * K :, cols]), split(x))
        y_ref[k * K :, :] = y if k == 0 else y_ref[k * K :, :] + y
        rhs[0][cols, where], rhs[1][cols, where] = split(y_ref[cols, :])


def end_step(meta, i, m_ref, lhs, rhs, pan, out):
    flat = out.reshape(F * T * 16, T)
    where = pl.ds(pl.multiple_of(i * F * T, F * T), F * T)
    left = lhs[0][where, :], lhs[1][where, :]
    for n in range(0, 2048, 512):
        cols = slice(n, n + 512)
        p = dot3(left, (rhs[0][:, cols], rhs[1][:, cols]))
        for a in range(F):
            for at in range(n // T, n // T + 4):
                lc = (at % 8) * 2 + at // 8
                flat[pl.ds(a * T * 16 + lc, T, stride=16), :] = (
                    m_ref[a, at] - p[a * T : (a + 1) * T, (at * T) % 512 : (at * T) % 512 + T]
                )
    for a in range(F):
        kept = (i * F + a == 0) & (meta[ROW_AT] < 4) & (meta[COL_AT] >= 4)

        @pl.when(jnp.logical_not(kept))
        def _():
            flat[pl.ds(a * T * 16, T, stride=16), :] = pan[i * F + a]


def finish_kernel(meta, ihi, ilo, x0, x1, x2, x3, xc, m_ref, out, lhi, llo, chi, clo, pan, xhi, xlo, yr, yc):
    i = pl.program_id(0)

    @pl.when(i < ROW_STEPS)
    def _():
        rows_step(meta, i, (ihi, ilo), (x0, x1, x2, x3), (lhi, llo), pan, (xhi, xlo), yr)

    @pl.when((i >= ROW_STEPS) & (i < ROW_STEPS + COL_STEPS))
    def _():
        cols_step(i - ROW_STEPS, (ihi, ilo), xc, (chi, clo), yc)

    @pl.when(i >= ROW_STEPS + COL_STEPS)
    def _():
        end_step(meta, i - ROW_STEPS - COL_STEPS, m_ref, (lhi, llo), (chi, clo), pan, out)


def finish(meta, inverse, rows_x, cols_x, m):
    def part(i, before, count):
        return jnp.clip(i - before, 0, count - 1)

    def col_block(i, m):
        j = part(i, ROW_STEPS, COL_STEPS)
        return j // (1024 // B), 0, j % (1024 // B), 0, 0

    def end_block(i, m):
        return part(i, ROW_STEPS + COL_STEPS, END_STEPS), 0, 0, 0

    whole = pl.BlockSpec((W, W), lambda i, m: (0, 0), pipeline_mode=pl.Buffered(1))
    tiles = pl.BlockSpec((2, H, T, T), lambda i, m: (0, part(i, 0, ROW_STEPS), 0, 0))
    return pl.pallas_call(
        finish_kernel,
        grid_spec=pltpu.PrefetchScalarGridSpec(
            num_scalar_prefetch=1,
            grid=(ROW_STEPS + COL_STEPS + END_STEPS,),
            in_specs=[whole, whole]
            + [tiles] * 4
            + [pl.BlockSpec((None, 8, B // T, T, T), col_block), pl.BlockSpec((F, 16, T, T), end_block)],
            out_specs=pl.BlockSpec((F, T, 16, T), end_block),
            scratch_shapes=[
                pltpu.VMEM((W, W), BF16),
                pltpu.VMEM((W, W), BF16),
                pltpu.VMEM((W, 2048), BF16),
                pltpu.VMEM((W, 2048), BF16),
                pltpu.VMEM((8, T, T), F32),
                pltpu.VMEM((H * T, W), BF16),
                pltpu.VMEM((H * T, W), BF16),
                pltpu.VMEM((H * T, W), F32),
                pltpu.VMEM((W, B), F32),
            ],
        ),
        out_shape=jax.ShapeDtypeStruct((8, T, 16, T), F32),
        compiler_params=params(),
        name="finish",
    )(meta, *inverse, *rows_x, cols_x, m)


def exchange(x, axis):
    return lax.all_to_all(x, axis, split_axis=0, concat_axis=0, tiled=True)


def row_id(y, z, core):
    return (y % 2) * 8 + (z % 4) * 2 + core % 2


def col_id(x, y):
    return (x % 4) * 2 + y % 2


def along_row(v, dy, dz, dcore):
    pairs = [
        (row_id(y, z, core), row_id(y + dy, z + dz, core + dcore))
        for y in range(2)
        for z in range(4)
        for core in range(2)
    ]
    return lax.ppermute(v, "row", pairs)


def along_col(v, dx, dy):
    return lax.ppermute(
        v, "col", [(col_id(x, y), col_id(x + dx, y + dy)) for x in range(4) for y in range(2)]
    )


def down(v):
    return lax.ppermute(v, "row", [(i, i + 8) for i in range(8)])


def shards(front, child_blocks, child_map):
    row = lax.axis_index("row")
    col = lax.axis_index("col")
    meta = jnp.concatenate([child_map.reshape(-1), jnp.stack([row, col])]).astype(jnp.int32)
    upper = row < 8

    arrived = exchange(pack_rows(meta, child_blocks), "row")
    landed = exchange(pack_cols(meta, arrived), "col")
    first = assemble(meta, front, landed, 0, 1)[0]

    tile = first[0]
    across = [(q * 8 + c, (q + 8) * 8 + (c ^ 1)) for q in range(8) for c in range(8)]
    two = jnp.where(
        upper,
        jnp.stack([tile, along_col(tile, 0, 1)]),
        jnp.stack([down(tile), lax.ppermute(tile, ("row", "col"), across)]),
    )
    two, first, landed, front = lax.optimization_barrier((two, first, landed, front))
    line = jnp.stack([two] + [along_col(two, dx, 0) for dx in (1, 2, 3)])
    ours = jnp.where(upper, first[:8], down(first[8:]))
    mine = first_col(meta, front, landed)
    line, mine, landed, front = lax.optimization_barrier((line, mine, landed, front))
    parts = [line] + [along_row(line, 0, dz, 0) for dz in (1, 2, 3)]
    pair = jnp.stack([mine, along_col(mine, 0, 1)])
    matrix = assemble(meta, front, landed, 0, 8)
    parts, pair, ours, matrix = lax.optimization_barrier((parts, pair, ours, matrix))
    own = jnp.stack(parts)
    other = along_row(own, 0, 0, 1)

    cols_x = lax.all_gather(ours, "row").reshape(2, 8, 8, T, T)
    other, pair = lax.optimization_barrier((other, pair))
    rows_x = [pair] + [along_col(pair, dx, 0) for dx in (1, 2, 3)]

    inverse = invert(meta, own, other)
    return finish(meta, inverse, rows_x, cols_x, matrix)


def solution(mesh):
    in_specs = (P(None, "row", None, "col"), P(None, None, "row", None, "col"), P())
    out_specs = P(None, "row", None, "col")
    return jax.shard_map(shards, mesh=mesh, in_specs=in_specs, out_specs=out_specs, check_vma=False)
```
